512 devices in a mesh: frame: 16 (over y, core), row: 32 (over x, z).
Axes of the slice: x: 4, y: 8, z: 8, core: 2. Of those that a mesh axis runs over, the one named last changes fastest.
Arguments:
- video_tail: bfloat16 [16, 32, 128, 256], P('frame', 'row'), may hold values from -6 to 6
- video_head: bfloat16 [32, 128, 256], P('row', 'frame'), may hold values from -6 to 6
- cotangent_tail: bfloat16 [16, 32, 128, 256], P('frame', 'row'), may hold values from -6 to 6
- cotangent_head: bfloat16 [32, 128, 256], P('row', 'frame'), may hold values from -6 to 6
- modulation: float32 [256], replicated, may hold values from 0.25 to 1.75
- conv_weight: bfloat16 [9, 256, 256], replicated, may hold values from -0.125 to 0.125
- conv_bias: float32 [256], replicated, may hold values from -3 to 3
- temporal_weight: bfloat16 [3, 256, 256], replicated, may hold values from -0.21875 to 0.21875
Outputs:
- grad_tail: bfloat16 [16, 32, 128, 256], P('frame', 'row')
- grad_head: bfloat16 [32, 128, 256], P('row', 'frame')
- grad_conv: float32 [9, 256, 256], P(None, 'row')
- grad_temporal: float32 [3, 256, 256], P(None, 'row')
- grad_vectors: float32 [2, 256], P(None, 'row')
The draws below stay inside these ranges and needn't reach their ends.
All inputs are finite; a program needn't handle non-finite values.
Results may differ from the reference program's by a relative error of at most 0.0061.
Values may be sent and summed in bfloat16 or wider, within the bound.
A program may use at most 64 MiB of HBM per device.

```python
import math
import jax
import jax.numpy as jnp
from jax import lax

C = 256
W = 128
FRAMES = 16
H = 32


def levels(own_key, dims, shards, low, top_value):
    gain, own = 1.0, jax.random.fold_in(own_key, 6)
    for axis_at, parts in shards:
        steps = jnp.exp(jax.random.uniform(jax.random.fold_in(own, axis_at), (parts,), jnp.float32, low / len(shards), top_value / len(shards)))
        gain = gain * jnp.repeat(steps, dims[axis_at] // parts).reshape([-1 if axis == axis_at else 1 for axis in range(len(dims))])
    return gain


def noise(rng, extent, width, most, shards=(), kind=jnp.bfloat16):
    values = jax.random.normal(rng, extent, jnp.float32) * width
    if len(shards) > 0:
        values = levels(rng, extent, shards, -0.22, 0.18) * values
    return jnp.clip(values, min=-most, max=most).astype(kind)


def setup_inputs(seed: int = 0) -> dict:
    key_of = jax.random.split(jax.random.key(seed), 9)
    video_tail = noise(key_of[0], (FRAMES, H, W, C), 1.0, 6.0, ((0, 16), (1, 32)))
    video_head = noise(key_of[1], (H, W, C), 1.0, 6.0, ((0, 32), (1, 16)))
    cotangent_tail = noise(key_of[2], (FRAMES, H, W, C), 1.0, 6.0, ((0, 16), (1, 32)))
    cotangent_head = noise(key_of[3], (H, W, C), 1.0, 6.0, ((0, 32), (1, 16)))
    modulation = jnp.clip(1.0 + 0.15 * jax.random.normal(key_of[4], (C,), jnp.float32), 0.25, 1.75)
    conv_weight = noise(key_of[5], (9, C, C), (9 * C) ** -0.5, 0.125)
    conv_bias = noise(key_of[6], (C,), 0.5, 3.0, (), jnp.float32)
    temporal_weight = noise(key_of[7], (3, C, C), (3 * C) ** -0.5, 0.21875)
    return dict(video_tail=video_tail, video_head=video_head, cotangent_tail=cotangent_tail, cotangent_head=cotangent_head, modulation=modulation, conv_weight=conv_weight, conv_bias=conv_bias, temporal_weight=temporal_weight)


def conv_frames(padded, kernel):
    count_frames, padded_rows, padded_cols, channels = padded.shape
    height = padded_rows - 2
    breadth = padded_cols - 2
    summed = jnp.zeros((count_frames * height * breadth, kernel.shape[2]), jnp.float32)
    for tap_index in range(9):
        tap_row = tap_index // 3
        tap_col = tap_index % 3
        window = padded[:, tap_row:tap_row + height, tap_col:tap_col + breadth].reshape(count_frames * height * breadth, channels)
        summed = summed + jnp.dot(window, kernel[tap_index], preferred_element_type=jnp.float32)
    return summed.reshape(count_frames, height, breadth, kernel.shape[2])

def weight_frames(padded, gradient):
    count_frames, height, breadth, channels = gradient.shape
    flattened = gradient.reshape(count_frames * height * breadth, channels)
    results = []
    for tap_index in range(9):
        tap_row = tap_index // 3
        tap_col = tap_index % 3
        window = padded[:, tap_row:tap_row + height, tap_col:tap_col + breadth].reshape(count_frames * height * breadth, padded.shape[3])
        results.append(lax.dot_general(window, flattened, (((0,), (0,)), ((), ())), preferred_element_type=jnp.float32))
    return jnp.stack(results)

def flipped(kernel):
    return jnp.transpose(kernel[::-1], (0, 2, 1))

def silu_slope(pre_act):
    sigmoid_val = jax.nn.sigmoid(pre_act)
    return sigmoid_val * (1.0 + pre_act * (1.0 - sigmoid_val))

def pad_frame(frames):
    return jnp.pad(frames, ((0, 0), (1, 1), (1, 1), (0, 0)))

def reference(video_tail, video_head, cotangent_tail, cotangent_head, modulation, conv_weight, conv_bias, temporal_weight):
    video_all = jnp.concatenate([video_head[None], video_tail], axis=0)
    cotangent = jnp.concatenate([cotangent_head[None], cotangent_tail], axis=0)
    norm_scale = 1.0 / math.sqrt((FRAMES + 1) * H * W)
    seq_len = FRAMES + 1

    def forward(frame_data):
        modulated = (frame_data.astype(jnp.float32) * modulation).astype(jnp.bfloat16)[None]
        pre_act = conv_frames(pad_frame(modulated), conv_weight)[0] + conv_bias
        return jax.nn.silu(pre_act).astype(jnp.bfloat16)
    activation = lax.map(forward, video_all)
    act_rows = activation.reshape(seq_len, H * W, C)
    cot_rows = cotangent.reshape(seq_len, H * W, C)
    dgrad = jnp.zeros((seq_len * H * W, C), jnp.float32)
    temporal_terms = []
    for lag_index in range(3):
        ahead = jnp.concatenate([cot_rows[lag_index:], jnp.zeros((lag_index, H * W, C), jnp.bfloat16)], axis=0).reshape(seq_len * H * W, C)
        behind = jnp.concatenate([jnp.zeros((lag_index, H * W, C), jnp.bfloat16), act_rows[:seq_len - lag_index]], axis=0).reshape(seq_len * H * W, C)
        dgrad = dgrad + lax.dot_general(ahead, temporal_weight[lag_index], (((1,), (1,)), ((), ())), preferred_element_type=jnp.float32)
        temporal_terms.append(lax.dot_general(behind, cot_rows.reshape(seq_len * H * W, C), (((0,), (0,)), ((), ())), preferred_element_type=jnp.float32))
    act_grad = dgrad.astype(jnp.bfloat16).reshape(seq_len, H, W, C)
    kernel_back = flipped(conv_weight)

    def backward(triples):
        frame_data, cot_frame, grad_frame = triples
        modulated = (frame_data.astype(jnp.float32) * modulation).astype(jnp.bfloat16)[None]
        padded = pad_frame(modulated)
        pre_act = conv_frames(padded, conv_weight)[0] + conv_bias
        pre_grad = (grad_frame.astype(jnp.float32) * silu_slope(pre_act)).astype(jnp.bfloat16)
        mod_grad = conv_frames(pad_frame(pre_grad[None]), kernel_back)[0]
        input_grad = (cot_frame.astype(jnp.float32) + modulation * mod_grad).astype(jnp.bfloat16)
        kernel_terms = weight_frames(padded, pre_grad[None])
        scale_terms = lax.optimization_barrier(jnp.sum(frame_data.astype(jnp.float32) * mod_grad, axis=(0, 1)))
        bias_terms = lax.optimization_barrier(jnp.sum(pre_grad.astype(jnp.float32), axis=(0, 1)))
        return (input_grad, kernel_terms, scale_terms, bias_terms)
    input_grad, kernel_terms, scale_terms, bias_terms = lax.map(backward, (video_all, cotangent, act_grad))
    grad_conv = lax.optimization_barrier(jnp.sum(kernel_terms, axis=0)) * norm_scale
    grad_temporal = jnp.stack(temporal_terms) * norm_scale
    grad_vectors = jnp.stack([lax.optimization_barrier(jnp.sum(scale_terms, axis=0)), lax.optimization_barrier(jnp.sum(bias_terms, axis=0))]) * norm_scale
    return (input_grad[1:], input_grad[0], grad_conv, grad_temporal, grad_vectors)
```

```python
import functools
import math

import jax
import jax.numpy as jnp
from jax import lax
from jax.experimental import pallas as pl
from jax.experimental.pallas import tpu as pltpu
from jax.sharding import PartitionSpec as P

MESH = pl.DeviceIdType.MESH
F32 = jnp.float32
BF16 = jnp.bfloat16
COLS = 128
CH = 256
HEAD = 8
ROWS = 160
NX, NY, NZ, NF, NR = 4, 8, 8, 16, 32
SCALE = 1.0 / math.sqrt(17 * 32 * 128)


class Slots:
    def __init__(self):
        self.count = 0

    def take(self, n):
        first = self.count
        self.count += n
        return first


S = Slots()
S_VROW, S_CNEXT, S_HV, S_CH = S.take(2), S.take(2), S.take(9), S.take(2)
S_PROW, S_PH = S.take(2), S.take(9)
S_PAIR = S.take(4)
S_X, S_Z, S_Y = S.take(9), S.take(7), S.take(7)
S_VZ, S_VX, S_VY = S.take(7), S.take(3), S.take(7)
S_CHSEND, S_VLAST = S.take(15), S.take(1)
N_SEM = S.count


def dot(a, b):
    return jnp.dot(a, b, preferred_element_type=F32)


def dot_back(a, b):
    return lax.dot_general(a, b, (((1,), (1,)), ((), ())), preferred_element_type=F32)


def dot_outer(a, b):
    return lax.dot_general(a, b, (((0,), (0,)), ((), ())), preferred_element_type=F32)


def down(v):
    return pltpu.roll(v, 1, 0)


def up(v):
    return pltpu.roll(v, v.shape[0] - 1, 0)


def kernel(
    vid_h, vh_h, cot_h, ch_h, mod_h, cw_h, cb_h, tw_h,
    gt_o, gh_o, gc_o, gtw_o, gv_o,
    vid, vh, cot, ch, mod, wv, cb, tw,
    vh32, cot32, vrow, cnext, hv, chs,
    left, lsib, right, back, prow, pgt, pgh, ph,
    prod, g, xb, h, zb, yb, total,
    vec, vzb, vxb, vyb, vpair,
    lsem, ss, rs,
):
    f = lax.axis_index("frame")
    r = lax.axis_index("row")
    y, c = lax.div(f, 2), lax.rem(f, 2)
    x, z = lax.div(r, NZ), lax.rem(r, NZ)

    def at(fo, ro):
        return (lax.rem(f + fo + NF, NF), lax.rem(r + ro + NR, NR))

    def at_x(o):
        return (f, lax.rem(x + o, NX) * NZ + z)

    def at_z(o):
        return (f, x * NZ + lax.rem(z + o, NZ))

    def at_y(o):
        return (lax.rem(y + o, NY) * 2 + c, r)

    sibling = (y * 2 + 1 - c, r)

    def remote(src, dst, send, recv, device):
        return pltpu.make_async_remote_copy(
            src_ref=src, dst_ref=dst, send_sem=ss.at[send], recv_sem=rs.at[recv],
            device_id=device, device_id_type=MESH,
        )

    pending = []

    def send(src, dst, slot, device):
        copy = remote(src, dst, slot, slot, device)
        copy.start()
        pending.append(copy)
        return copy

    pairs = [
        (vid_h, vid), (cot_h, cot), (vh_h, vh), (ch_h, ch), (mod_h, mod), (cb_h, cb),
    ] + [(cw_h.at[:, q], wv.at[q]) for q in range(3)] + [(tw_h, tw)]
    local = [pltpu.make_async_copy(a, b, lsem.at[i]) for i, (a, b) in enumerate(pairs)]
    for copy in local:
        copy.start()

    barrier = pltpu.get_barrier_semaphore()
    partners = [at(o, 0) for o in range(1, NF)]
    partners += [at_x(o) for o in range(1, NX)] + [at_z(o) for o in range(1, NZ)]
    partners += [at(fo, ro) for fo in (-1, 0, 1) for ro in (-1, 1)]
    for device in partners:
        pl.semaphore_signal(barrier, inc=1, device_id=device, device_id_type=MESH)

    for copy in local[:6]:
        copy.wait()
    vh32[...] = vh[...].astype(F32)
    cot32[...] = cot[...].astype(F32).reshape(NF, HEAD, CH)
    pl.semaphore_wait(barrier, len(partners))

    send(vid, vrow.at[0], S_VROW, at(0, 1))
    send(vid, vrow.at[1], S_VROW + 1, at(0, -1))
    around = [(dr, dc) for dr in (-1, 0, 1) for dc in (-1, 0, 1) if (dr, dc) != (0, 0)]

    def slot_of(dr, dc):
        return 3 * (dr + 1) + dc + 1

    for dr, dc in around:
        k = slot_of(dr, dc)
        send(vh32, hv.at[k], S_HV + k, at(-dc, -dr))
    send(cot, cnext.at[0], S_CNEXT, at(-1, 0))
    send(cot, cnext.at[1], S_CNEXT + 1, at(-2, 0))

    def head_cot(o):
        to = lax.rem(f + o, NF)
        return remote(cot32.at[to], chs.at[f], S_CHSEND + o - 1, S_CH + f, (to, r))

    @pl.when(f < 2)
    def _():
        for o in range(1, NF):
            head_cot(o).start()
        chs[f] = cot32[f]

    n_first = len(pending)
    for copy in pending[: n_first - 2]:
        copy.wait_recv()
    row_ids = lax.broadcasted_iota(jnp.int32, (HEAD, CH), 0)
    zero8 = jnp.zeros((HEAD, CH), F32)
    modv = mod[...]

    def row_ok(dr):
        return (r + dr >= 0) & (r + dr < NR)

    def head_block(own, pieces, dr, factor):
        ok_prev = f > 0
        ok_next = f < NF - 1
        if dr != 0:
            ok_prev = ok_prev & row_ok(dr)
            ok_next = ok_next & row_ok(dr)
        prev = jnp.where((row_ids == HEAD - 1) & ok_prev, pieces[slot_of(dr, -1)], 0.0)
        after = jnp.where((row_ids == 0) & ok_next, pieces[slot_of(dr, 1)], 0.0)
        mid = own if dr == 0 else jnp.where(row_ok(dr), pieces[slot_of(dr, 0)], 0.0)
        block = jnp.concatenate([prev, mid, after, zero8], axis=0)
        return (block * factor).astype(BF16) if factor is not None else block.astype(BF16)

    for p in range(3):
        dr = p - 1
        rows = vid[...] if dr == 0 else vrow[0 if dr < 0 else 1]
        factor = modv if dr == 0 else jnp.where(row_ok(dr), modv, 0.0)
        left[0:COLS, p * CH : (p + 1) * CH] = (rows.astype(F32) * factor).astype(BF16)
        left[COLS:ROWS, p * CH : (p + 1) * CH] = head_block(vh32[...], hv, dr, modv)

    for copy in local[6:]:
        copy.wait()

    xs = left[:, 0 : 3 * CH]
    pre = down(dot(xs, wv[0].reshape(3 * CH, CH)))
    pre = pre + dot(xs, wv[1].reshape(3 * CH, CH))
    pre = pre + up(dot(xs, wv[2].reshape(3 * CH, CH)))
    pre = pre + cb[...]
    sig = jax.nn.sigmoid(pre)
    left[:, 3 * CH : 4 * CH] = (pre * sig).astype(BF16)
    slope = sig * (1.0 + pre * (1.0 - sig))

    half_other = pl.multiple_of(2 * CH * (1 - c), 2 * CH)
    half_mine = pl.multiple_of(2 * CH * c, 2 * CH)
    send_l = send(left.at[:, pl.ds(half_other, 2 * CH)], lsib.at[1], S_PAIR, sibling)

    for copy in pending[n_first - 2 : n_first]:
        copy.wait_recv()
    for s in range(2):

        @pl.when(f != s)
        def _():
            remote(cot32.at[0], chs.at[s], S_CHSEND, S_CH + s, sibling).wait_recv()

    grad = None
    for k in range(3):
        if k == 0:
            tail, head = cot[...], ch[...].astype(F32)
        else:
            tail = jnp.where(f + k < NF, cnext[k - 1].astype(F32), 0.0).astype(BF16)
            head = chs[k - 1]
        right[1, 0, 0:COLS, k * CH : (k + 1) * CH] = tail
        right[1, 0, COLS:ROWS, k * CH : (k + 1) * CH] = jnp.concatenate(
            [zero8, head, zero8, zero8], axis=0
        ).astype(BF16)
        term = dot_back(right[1, 0, :, k * CH : (k + 1) * CH], tw[k])
        grad = term if grad is None else grad + term
    send_c = send(right.at[1, 0], right.at[1, 1], S_PAIR + 1, sibling)

    pg16 = (grad.astype(BF16).astype(F32) * slope).astype(BF16)
    pg = pg16.astype(F32)
    right[0, 0, :, 0:CH] = up(pg).astype(BF16)
    right[0, 0, :, CH : 2 * CH] = pg16
    right[0, 0, :, 2 * CH : 3 * CH] = down(pg).astype(BF16)
    send_p = send(right.at[0, 0], right.at[0, 1], S_PAIR + 2, sibling)
    pgt[...] = pg16[0:COLS]
    pgh[...] = pg[COLS + HEAD : COLS + 2 * HEAD]
    second = [send(pgt, prow.at[0], S_PROW, at(0, 1)), send(pgt, prow.at[1], S_PROW + 1, at(0, -1))]
    for dr, dc in around:
        k = slot_of(dr, dc)
        second.append(send(pgh, ph.at[k], S_PH + k, at(-dc, -dr)))
    bias_terms = jnp.sum(pg, axis=0, keepdims=True)

    lsib[0] = left[:, pl.ds(half_mine, 2 * CH)]
    send_l.wait_recv()
    send_c.wait_recv()
    send_p.wait_recv()
    xsends = {}
    for j in (1, 0):
        lhs = lsib[:, :, j * CH : (j + 1) * CH].reshape(2 * ROWS, CH)
        rhs = right[0 if j == 0 else c].reshape(2 * ROWS, 3 * CH)
        prod[j] = dot_outer(lhs, rhs)
        for t in (2,) if j == 1 else (0, 1):
            parts = [
                prod[tap // 3, :, (tap % 3) * CH : (tap % 3 + 1) * CH].reshape(NX, NZ, 8, CH)
                for tap in (2 * t, 2 * t + 1)
            ]
            g[t] = jnp.concatenate(parts, axis=2).astype(BF16)
            for o in range(1, NX):
                slot = 3 * t + o - 1
                to = lax.rem(x + o, NX)
                xsends[t, o] = send(g.at[t, to], xb.at[t, o - 1], S_X + slot, at_x(o))

    for copy in second:
        copy.wait_recv()
    for p in range(3):
        dr = 1 - p
        if dr == 0:
            rows = pgt[...]
        else:
            rows = prow[0 if dr < 0 else 1].astype(F32)
            rows = jnp.where(row_ok(dr), rows, 0.0).astype(BF16)
        back[p, 0:COLS, :] = rows
        back[p, COLS:ROWS, :] = head_block(pgh[...], ph, dr, None)
    convs = []
    for q in range(3):
        acc = None
        for p in range(3):
            term = dot_back(back[p], wv[q, p])
            acc = term if acc is None else acc + term
        convs.append(acc)
    mod_grad = up(convs[0]) + convs[1] + down(convs[2])
    tail_grad = mod_grad[0:COLS]
    head_grad = mod_grad[COLS + HEAD : COLS + 2 * HEAD]
    gt_o[...] = (cot[...].astype(F32) + modv * tail_grad).astype(BF16)
    gh_o[...] = (ch[...].astype(F32) + modv * head_grad).astype(BF16)
    scale_terms = jnp.sum(vid[...].astype(F32) * tail_grad, axis=0, keepdims=True)
    scale_terms = scale_terms + jnp.sum(vh32[...] * head_grad, axis=0, keepdims=True)
    vec[0] = jnp.concatenate(
        [
            scale_terms[:, 0:128], scale_terms[:, 128:256],
            bias_terms[:, 0:128], bias_terms[:, 128:256],
            jnp.zeros((4, 128), F32),
        ],
        axis=0,
    )
    vz = [send(vec.at[0], vzb.at[o - 1], S_VZ + o - 1, at_z(o)) for o in range(1, NZ)]

    for t in (2, 0, 1):
        acc = g[t, x].astype(F32)
        for o in range(1, NX):
            xsends[t, o].wait_recv()
            acc = acc + xb[t, o - 1].astype(F32)
        h[:, t] = acc.astype(BF16)
    zsends = []
    for o in range(1, NZ):
        zsends.append(send(h.at[lax.rem(z + o, NZ)], zb.at[o - 1], S_Z + o - 1, at_z(o)))
    acc = vec[0]
    for o in range(1, NZ):
        vz[o - 1].wait_recv()
        acc = acc + vzb[o - 1]
    vec[1] = acc
    vx = [send(vec.at[1], vxb.at[o - 1], S_VX + o - 1, at_x(o)) for o in range(1, NX)]
    acc = h[z].astype(F32)
    for o in range(1, NZ):
        zsends[o - 1].wait_recv()
        acc = acc + zb[o - 1].astype(F32)
    yb[y] = acc.astype(BF16)
    ysends = [send(yb.at[y], yb.at[y], S_Y + o - 1, at_y(o)) for o in range(1, NY)]
    acc = vec[1]
    for o in range(1, NX):
        vx[o - 1].wait_recv()
        acc = acc + vxb[o - 1]
    vyb[y] = acc
    vy = [send(vyb.at[y], vyb.at[y], S_VY + o - 1, at_y(o)) for o in range(1, NY)]
    for o in range(1, NY):
        from_y = lax.rem(y + NY - o, NY)
        remote(yb.at[from_y], yb.at[from_y], S_Y + o - 1, S_Y + o - 1, sibling).wait_recv()
        remote(vyb.at[from_y], vyb.at[from_y], S_VY + o - 1, S_VY + o - 1, sibling).wait_recv()
    acc = yb[0].astype(F32)
    vacc = vyb[0]
    for s in range(1, NY):
        acc = acc + yb[s].astype(F32)
        vacc = vacc + vyb[s]
    total[pl.ds(6 * c, 6)] = (acc * SCALE).reshape(6, 8, CH)
    vpair[0] = vacc
    mine = total.at[pl.ds(6 * c, 6)]
    theirs = total.at[pl.ds(6 * (1 - c), 6)]
    last = send(mine, mine, S_PAIR + 3, sibling)
    vlast = send(vpair.at[0], vpair.at[1], S_VLAST, sibling)
    remote(theirs, theirs, S_PAIR + 3, S_PAIR + 3, sibling).wait_recv()
    vlast.wait_recv()
    gc_o[...] = total[0:9]
    gtw_o[...] = total[9:12]
    both = (vpair[0] + vpair[1]) * SCALE
    low = r < NR // 2
    two = jnp.concatenate(
        [
            jnp.where(low, both[0:1], both[1:2]),
            jnp.where(low, both[2:3], both[3:4]),
            jnp.zeros((6, 128), F32),
        ],
        axis=0,
    )
    turned = pltpu.roll(two, lax.rem(128 - 8 * lax.rem(r, 16), 128), 1)
    gv_o[...] = turned[0:2, 0:8]

    for copy in pending:
        copy.wait_send()

    @pl.when(f < 2)
    def _():
        for o in range(1, NF):
            head_cot(o).wait_send()


def body(video_tail, video_head, cotangent_tail, cotangent_head, modulation, conv_weight, conv_bias, temporal_weight):
    any_spec = pl.BlockSpec(memory_space=pl.ANY)
    vmem = pl.BlockSpec(memory_space=pltpu.VMEM)
    scratch = [
        ((COLS, CH), BF16), ((HEAD, CH), BF16), ((COLS, CH), BF16), ((HEAD, CH), BF16),
        ((1, CH), F32), ((3, 3, CH, CH), BF16), ((1, CH), F32), ((3, CH, CH), BF16),
        ((HEAD, CH), F32), ((NF, HEAD, CH), F32), ((2, COLS, CH), BF16), ((2, COLS, CH), BF16),
        ((9, HEAD, CH), F32), ((2, HEAD, CH), F32),
        ((ROWS, 4 * CH), BF16), ((2, ROWS, 2 * CH), BF16), ((2, 2, ROWS, 3 * CH), BF16),
        ((3, ROWS, CH), BF16), ((2, COLS, CH), BF16), ((COLS, CH), BF16), ((HEAD, CH), F32),
        ((9, HEAD, CH), F32),
        ((2, CH, 3 * CH), F32), ((3, NX, NZ, 16, CH), BF16), ((3, NX - 1, NZ, 16, CH), BF16),
        ((NZ, 3, 16, CH), BF16), ((NZ - 1, 3, 16, CH), BF16), ((NY, 3, 16, CH), BF16),
        ((12, 8, CH), F32),
        ((2, 8, 128), F32), ((NZ - 1, 8, 128), F32), ((NX - 1, 8, 128), F32), ((NY, 8, 128), F32),
        ((2, 8, 128), F32),
    ]
    outs = pl.pallas_call(
        kernel,
        out_shape=(
            jax.ShapeDtypeStruct((COLS, CH), BF16),
            jax.ShapeDtypeStruct((HEAD, CH), BF16),
            jax.ShapeDtypeStruct((9, 8, CH), F32),
            jax.ShapeDtypeStruct((3, 8, CH), F32),
            jax.ShapeDtypeStruct((2, 8), F32),
        ),
        in_specs=[any_spec] * 8,
        out_specs=(vmem,) * 5,
        scratch_shapes=[pltpu.VMEM(shape, kind) for shape, kind in scratch]
        + [
            pltpu.SemaphoreType.DMA((10,)),
            pltpu.SemaphoreType.DMA((N_SEM,)),
            pltpu.SemaphoreType.DMA((N_SEM,)),
        ],
        compiler_params=pltpu.CompilerParams(
            collective_id=0, has_side_effects=True, vmem_limit_bytes=48 << 20
        ),
        name="video_block_backward",
    )(
        video_tail.reshape(COLS, CH),
        video_head.reshape(HEAD, CH),
        cotangent_tail.reshape(COLS, CH),
        cotangent_head.reshape(HEAD, CH),
        modulation.reshape(1, CH),
        conv_weight.reshape(3, 3, CH, CH),
        conv_bias.reshape(1, CH),
        temporal_weight,
    )
    return (outs[0].reshape(1, 1, COLS, CH), outs[1].reshape(1, HEAD, CH), outs[2], outs[3], outs[4])


def solution(mesh):
    return jax.shard_map(
        body,
        mesh=mesh,
        in_specs=(
            P("frame", "row", None, None),
            P("row", "frame", None),
            P("frame", "row", None, None),
            P("row", "frame", None),
            P(),
            P(),
            P(),
            P(),
        ),
        out_specs=(
            P("frame", "row", None, None),
            P("row", "frame", None),
            P(None, "row", None),
            P(None, "row", None),
            P(None, "row"),
        ),
        check_vma=False,
    )
```

```python
import functools
import math

import jax
import jax.numpy as jnp
from jax import lax
from jax.experimental import pallas as pl
from jax.experimental.pallas import tpu as pltpu
from jax.sharding import PartitionSpec as P

MESH = pl.DeviceIdType.MESH
F32 = jnp.float32
BF16 = jnp.bfloat16
COLS = 128
CH = 256
HEAD = 8
ROWS = 160
NX, NY, NZ, NF, NR = 4, 8, 8, 16, 32
SCALE = 1.0 / math.sqrt(17 * 32 * 128)


GROUPS = (
    "vrow", "cnext", "hv", "ch0", "ch1", "prow", "ph", "lsib", "csib", "psib", "total",
    "x0", "x1", "z", "zf", "xl", "y", "vz", "vx", "vy", "vpair",
)
SEM = {name: i for i, name in enumerate(GROUPS)}


def stacked(piece):
    half = CH // 2
    return jnp.concatenate([piece[..., :half], piece[..., half:]], axis=-2).astype(BF16)


def unstacked(piece):
    rows = piece.astype(F32)
    return jnp.concatenate([rows[:HEAD], rows[HEAD:]], axis=1)


def dot(a, b):
    return jnp.dot(a, b, preferred_element_type=F32)


def dot_back(a, b):
    return lax.dot_general(a, b, (((1,), (1,)), ((), ())), preferred_element_type=F32)


def dot_outer(a, b):
    return lax.dot_general(a, b, (((0,), (0,)), ((), ())), preferred_element_type=F32)


def down(v):
    return pltpu.roll(v, 1, 0)


def up(v):
    return pltpu.roll(v, v.shape[0] - 1, 0)


def kernel(
    vid_h, vh_h, cot_h, ch_h, mod_h, cw_h, cb_h, tw_h,
    gt_o, gh_o, gc_o, gtw_o, gv_o,
    vc, heads, vecs, wv, tw, gt_v, gh_v, gc_v, gtw_v, gv_v,
    vhs, cots, vrow, cnext, hv, chs,
    left, lsib, right, back, prow, pgt, pgh, ph,
    prod, g, xb, h, zb, gz, zfb, hx, xlb, yb, total,
    vec, vzb, vxb, vyb, vpair,
    lsem, ss, rs,
):
    f = lax.axis_index("frame")
    r = lax.axis_index("row")
    y, c = lax.div(f, 2), lax.rem(f, 2)
    x, z = lax.div(r, NZ), lax.rem(r, NZ)

    def at(fo, ro):
        return (lax.rem(f + fo + NF, NF), lax.rem(r + ro + NR, NR))

    def at_x(o):
        return (f, lax.rem(x + o, NX) * NZ + z)

    def at_z(o):
        return (f, x * NZ + lax.rem(z + o, NZ))

    def at_y(o):
        return (lax.rem(y + o, NY) * 2 + c, r)

    sibling = (y * 2 + 1 - c, r)

    def remote(src, dst, sem, device):
        return pltpu.make_async_remote_copy(
            src_ref=src, dst_ref=dst, send_sem=ss.at[sem], recv_sem=rs.at[sem],
            device_id=device, device_id_type=MESH,
        )

    sent = {}

    def send(src, dst, name, device, whole):
        remote(src, dst, SEM[name], device).start()
        sent[name] = whole

    def arrived(name):
        whole = sent[name]
        remote(whole, whole, SEM[name], sibling).wait_recv()

    barrier = pltpu.get_barrier_semaphore()
    partners = [at(fo, ro) for ro in (-1, 1) for fo in (0, -1, 1)]
    partners += [at(o, 0) for o in range(1, NF)]
    partners += [at_x(o) for o in range(1, NX)] + [at_z(o) for o in range(1, NZ)]
    for device in partners:
        pl.semaphore_signal(barrier, inc=1, device_id=device, device_id_type=MESH)

    def local(group, src, dst):
        return pltpu.make_async_copy(src, dst, lsem.at[group])

    for group, src, dst in (
        (0, vid_h, vc.at[0]), (0, cot_h, vc.at[1]), (1, vh_h, heads.at[0]), (1, ch_h, heads.at[1]),
        (2, mod_h, vecs.at[0]), (2, cb_h, vecs.at[1]),
        (3, cw_h.at[:, 0], wv.at[0]), (3, cw_h.at[:, 1], wv.at[1]), (3, cw_h.at[:, 2], wv.at[2]),
        (4, tw_h, tw),
    ):
        local(group, src, dst).start()
    for group, whole in ((1, heads), (0, vc), (2, vecs)):
        local(group, whole, whole).wait()
    vid, cot = vc.at[0], vc.at[1]
    vh32, ch32 = heads[0].astype(F32), heads[1].astype(F32)
    vhs[...] = stacked(vh32)
    cots[...] = stacked(cot[...].astype(F32).reshape(NF, HEAD, CH))
    pl.semaphore_wait(barrier, len(partners))

    around = [(dr, dc) for dr in (0, -1, 1) for dc in (0, -1, 1) if (dr, dc) != (0, 0)]

    def slot_of(dr, dc):
        return (3 * dr + dc + 9) % 9 - 1

    for dr, dc in around:
        send(vhs, hv.at[slot_of(dr, dc)], "hv", at(-dc, -dr), hv)
    send(vid, vrow.at[0], "vrow", at(0, 1), vrow)
    send(vid, vrow.at[1], "vrow", at(0, -1), vrow)

    def head_cot(o):
        to = lax.rem(f + o, NF)
        return remote(cots.at[to], chs.at[f], SEM["ch0"] + f, (to, r))

    @pl.when(f < 2)
    def _():
        for o in range(1, NF):
            head_cot(o).start()
        chs[f] = cots[f]

    send(cot, cnext.at[0], "cnext", at(-1, 0), cnext)
    send(cot, cnext.at[1], "cnext", at(-2, 0), cnext)

    arrived("hv")
    arrived("vrow")
    row_ids = lax.broadcasted_iota(jnp.int32, (HEAD, CH), 0)
    zero8 = jnp.zeros((HEAD, CH), F32)
    modv = vecs[0]

    def row_ok(dr):
        return (r + dr >= 0) & (r + dr < NR)

    def head_block(own, pieces, dr, factor):
        ok_prev = f > 0
        ok_next = f < NF - 1
        if dr != 0:
            ok_prev = ok_prev & row_ok(dr)
            ok_next = ok_next & row_ok(dr)
        prev = jnp.where((row_ids == HEAD - 1) & ok_prev, unstacked(pieces[slot_of(dr, -1)]), 0.0)
        after = jnp.where((row_ids == 0) & ok_next, unstacked(pieces[slot_of(dr, 1)]), 0.0)
        mid = own if dr == 0 else jnp.where(row_ok(dr), unstacked(pieces[slot_of(dr, 0)]), 0.0)
        block = jnp.concatenate([prev, mid, after, zero8], axis=0)
        return (block * factor).astype(BF16) if factor is not None else block.astype(BF16)

    for p in range(3):
        dr = p - 1
        rows = vid[...] if dr == 0 else vrow[0 if dr < 0 else 1]
        factor = modv if dr == 0 else jnp.where(row_ok(dr), modv, 0.0)
        left[0:COLS, p * CH : (p + 1) * CH] = (rows.astype(F32) * factor).astype(BF16)
        left[COLS:ROWS, p * CH : (p + 1) * CH] = head_block(vh32, hv, dr, modv)

    local(3, wv, wv).wait()
    local(4, tw, tw).wait()

    xs = left[:, 0 : 3 * CH]
    pre = down(dot(xs, wv[0].reshape(3 * CH, CH)))
    pre = pre + dot(xs, wv[1].reshape(3 * CH, CH))
    pre = pre + up(dot(xs, wv[2].reshape(3 * CH, CH)))
    pre = pre + vecs[1]
    sig = jax.nn.sigmoid(pre)
    left[:, 3 * CH : 4 * CH] = (pre * sig).astype(BF16)
    slope = sig * (1.0 + pre * (1.0 - sig))

    half_other = pl.multiple_of(2 * CH * (1 - c), 2 * CH)
    half_mine = pl.multiple_of(2 * CH * c, 2 * CH)
    send(left.at[:, pl.ds(half_other, 2 * CH)], lsib.at[1], "lsib", sibling, lsib.at[1])

    arrived("cnext")
    for s in range(2):

        @pl.when(f != s)
        def _():
            remote(chs.at[s], chs.at[s], SEM["ch0"] + s, sibling).wait_recv()

    grad = None
    for k in range(3):
        if k == 0:
            tail, head = cot[...], ch32
        else:
            tail = jnp.where(f + k < NF, cnext[k - 1].astype(F32), 0.0).astype(BF16)
            head = unstacked(chs[k - 1])
        right[1, 0, 0:COLS, k * CH : (k + 1) * CH] = tail
        right[1, 0, COLS:ROWS, k * CH : (k + 1) * CH] = jnp.concatenate(
            [zero8, head, zero8, zero8], axis=0
        ).astype(BF16)
        term = dot_back(right[1, 0, :, k * CH : (k + 1) * CH], tw[k])
        grad = term if grad is None else grad + term
    send(right.at[1, 0], right.at[1, 1], "csib", sibling, right.at[1, 1])

    pg16 = (grad.astype(BF16).astype(F32) * slope).astype(BF16)
    pg = pg16.astype(F32)
    right[0, 0, :, CH : 2 * CH] = pg16
    theirs = right.at[0, 1, :, pl.ds(CH, CH)]
    send(right.at[0, 0, :, pl.ds(CH, CH)], theirs, "psib", sibling, theirs)
    pgt[...] = pg16[0:COLS]
    pg_head = pg[COLS + HEAD : COLS + 2 * HEAD]
    pgh[...] = stacked(pg_head)
    send(pgt, prow.at[0], "prow", at(0, 1), prow)
    send(pgt, prow.at[1], "prow", at(0, -1), prow)
    for dr, dc in around:
        send(pgh, ph.at[slot_of(dr, dc)], "ph", at(-dc, -dr), ph)
    right[0, 0, :, 0:CH] = up(pg).astype(BF16)
    right[0, 0, :, 2 * CH : 3 * CH] = down(pg).astype(BF16)
    bias_terms = jnp.sum(pg, axis=0, keepdims=True)

    lsib[0] = left[:, pl.ds(half_mine, 2 * CH)]
    arrived("lsib")
    arrived("csib")
    arrived("psib")
    other = right[0, 1, :, CH : 2 * CH].astype(F32)
    right[0, 1, :, 0:CH] = up(other).astype(BF16)
    right[0, 1, :, 2 * CH : 3 * CH] = down(other).astype(BF16)
    def pair_of_taps(t):
        parts = [
            prod[tap // 3, :, (tap % 3) * CH : (tap % 3 + 1) * CH].reshape(NX, NZ, 8, CH)
            for tap in (2 * t, 2 * t + 1)
        ]
        return jnp.concatenate(parts, axis=2).astype(BF16)

    for j in (1, 0):
        lhs = lsib[:, :, j * CH : (j + 1) * CH].reshape(2 * ROWS, CH)
        rhs = right[0 if j == 0 else c].reshape(2 * ROWS, 3 * CH)
        prod[j] = dot_outer(lhs, rhs)
        if j == 1:
            block = pair_of_taps(2)
            for i in range(NX):
                gz[:, i] = block[i]
            for o in range(1, NZ):
                to = lax.rem(z + o, NZ)
                send(gz.at[to], zfb.at[o - 1], "zf", at_z(o), zfb)
            continue
        for t in (0, 1):
            g[t] = pair_of_taps(t)
            for o in range(1, NX):
                to = lax.rem(x + o, NX)
                send(g.at[t, to], xb.at[t, o - 1], f"x{t}", at_x(o), xb.at[t])

    arrived("prow")
    arrived("ph")
    for p in range(3):
        dr = 1 - p
        if dr == 0:
            rows = pgt[...]
        else:
            rows = prow[0 if dr < 0 else 1].astype(F32)
            rows = jnp.where(row_ok(dr), rows, 0.0).astype(BF16)
        back[p, 0:COLS, :] = rows
        back[p, COLS:ROWS, :] = head_block(pg_head, ph, dr, None)
    convs = []
    for q in range(3):
        acc = None
        for p in range(3):
            term = dot_back(back[p], wv[q, p])
            acc = term if acc is None else acc + term
        convs.append(acc)
    mod_grad = up(convs[0]) + convs[1] + down(convs[2])
    tail_grad = mod_grad[0:COLS]
    head_grad = mod_grad[COLS + HEAD : COLS + 2 * HEAD]
    gt_v[...] = (cot[...].astype(F32) + modv * tail_grad).astype(BF16)
    gh_v[...] = (ch32 + modv * head_grad).astype(BF16)
    results = ((gt_v, gt_o), (gh_v, gh_o), (gc_v, gc_o), (gtw_v, gtw_o), (gv_v, gv_o))
    for i, (src, dst) in enumerate(results[:2]):
        local(i, src, dst).start()
    scale_terms = jnp.sum(vid[...].astype(F32) * tail_grad, axis=0, keepdims=True)
    scale_terms = scale_terms + jnp.sum(vh32 * head_grad, axis=0, keepdims=True)
    vec[0] = jnp.concatenate(
        [
            scale_terms[:, 0:128], scale_terms[:, 128:256],
            bias_terms[:, 0:128], bias_terms[:, 128:256],
            jnp.zeros((4, 128), F32),
        ],
        axis=0,
    )
    for o in range(1, NZ):
        send(vec.at[0], vzb.at[o - 1], "vz", at_z(o), vzb)

    def total_of(own, parts, count):
        acc = own.astype(F32)
        for i in range(count):
            acc = acc + parts[i].astype(F32)
        return acc

    for t in range(2):
        arrived(f"x{t}")
        h[:, t] = total_of(g[t, x], xb.at[t], NX - 1).astype(BF16)
    for o in range(1, NZ):
        send(h.at[lax.rem(z + o, NZ)], zb.at[o - 1], "z", at_z(o), zb)
    arrived("zf")
    hx[...] = total_of(gz[z], zfb, NZ - 1).astype(BF16)
    for o in range(1, NX):
        send(hx.at[lax.rem(x + o, NX)], xlb.at[o - 1], "xl", at_x(o), xlb)
    arrived("vz")
    vec[1] = total_of(vec[0], vzb, NZ - 1)
    for o in range(1, NX):
        send(vec.at[1], vxb.at[o - 1], "vx", at_x(o), vxb)
    arrived("xl")
    yb[y, 2] = total_of(hx[x], xlb, NX - 1).astype(BF16)
    arrived("z")
    yb[y, 0:2] = total_of(h[z], zb, NZ - 1).astype(BF16)
    for o in range(1, NY):
        send(yb.at[y], yb.at[y], "y", at_y(o), yb.at[pl.ds(0, NY - 1)])
    arrived("vx")
    vyb[y] = total_of(vec[1], vxb, NX - 1)
    for o in range(1, NY):
        send(vyb.at[y], vyb.at[y], "vy", at_y(o), vyb.at[pl.ds(0, NY - 1)])
    arrived("y")
    arrived("vy")
    acc = yb[0].astype(F32)
    vacc = vyb[0]
    for s in range(1, NY):
        acc = acc + yb[s].astype(F32)
        vacc = vacc + vyb[s]
    total[pl.ds(6 * c, 6)] = (acc * SCALE).reshape(6, 8, CH)
    vpair[0] = vacc
    mine = total.at[pl.ds(6 * c, 6)]
    send(mine, mine, "total", sibling, mine)
    send(vpair.at[0], vpair.at[1], "vpair", sibling, vpair.at[1])
    arrived("total")
    arrived("vpair")
    gc_v[...] = total[0:9]
    gtw_v[...] = total[9:12]
    both = (vpair[0] + vpair[1]) * SCALE
    low = r < NR // 2
    two = jnp.concatenate(
        [
            jnp.where(low, both[0:1], both[1:2]),
            jnp.where(low, both[2:3], both[3:4]),
            jnp.zeros((6, 128), F32),
        ],
        axis=0,
    )
    turned = pltpu.roll(two, lax.rem(128 - 8 * lax.rem(r, 16), 128), 1)
    gv_v[...] = turned[0:2, 0:8]
    for i, (src, dst) in enumerate(results[2:]):
        local(2 + i, src, dst).start()

    for name, whole in sent.items():
        remote(whole, whole, SEM[name], sibling).wait_send()

    @pl.when(f < 2)
    def _():
        whole = cots.at[pl.ds(0, NF - 1)]
        remote(whole, whole, SEM["ch0"] + f, sibling).wait_send()

    for i, (src, dst) in enumerate(results):
        local(i, src, dst).wait()


def write_out(*refs):
    sems = refs[10]
    copies = [pltpu.make_async_copy(refs[i], refs[5 + i], sems.at[i]) for i in range(5)]
    for copy in copies:
        copy.start()
    for copy in copies:
        copy.wait()


def body(video_tail, video_head, cotangent_tail, cotangent_head, modulation, conv_weight, conv_bias, temporal_weight):
    any_spec = pl.BlockSpec(memory_space=pl.ANY)
    scratch = [
        ((2, COLS, CH), BF16), ((2, HEAD, CH), BF16), ((2, 1, CH), F32),
        ((3, 3, CH, CH), BF16), ((3, CH, CH), BF16),
        ((COLS, CH), BF16), ((HEAD, CH), BF16), ((9, 8, CH), F32), ((3, 8, CH), F32), ((2, 8), F32),
        ((16, 128), BF16), ((NF, 16, 128), BF16), ((2, COLS, CH), BF16), ((2, COLS, CH), BF16),
        ((8, 16, 128), BF16), ((2, 16, 128), BF16),
        ((ROWS, 4 * CH), BF16), ((2, ROWS, 2 * CH), BF16), ((2, 2, ROWS, 3 * CH), BF16),
        ((3, ROWS, CH), BF16), ((2, COLS, CH), BF16), ((COLS, CH), BF16), ((16, 128), BF16),
        ((8, 16, 128), BF16),
        ((2, CH, 3 * CH), F32), ((2, NX, NZ, 16, CH), BF16), ((2, NX - 1, NZ, 16, CH), BF16),
        ((NZ, 2, 16, CH), BF16), ((NZ - 1, 2, 16, CH), BF16),
        ((NZ, NX, 16, CH), BF16), ((NZ - 1, NX, 16, CH), BF16), ((NX, 16, CH), BF16),
        ((NX - 1, 16, CH), BF16), ((NY, 3, 16, CH), BF16),
        ((12, 8, CH), F32),
        ((2, 8, 128), F32), ((NZ - 1, 8, 128), F32), ((NX - 1, 8, 128), F32), ((NY, 8, 128), F32),
        ((2, 8, 128), F32),
    ]
    shapes = [((COLS, CH), BF16), ((HEAD, CH), BF16), ((9, 8, CH), F32), ((3, 8, CH), F32), ((2, 8), F32)]
    operands = [
        video_tail.reshape(COLS, CH),
        video_head.reshape(HEAD, CH),
        cotangent_tail.reshape(COLS, CH),
        cotangent_head.reshape(HEAD, CH),
        modulation.reshape(1, CH),
        conv_weight.reshape(3, 3, CH, CH),
        conv_bias.reshape(1, CH),
        temporal_weight,
    ]
    outs = pl.pallas_call(
        kernel,
        out_shape=tuple(pltpu.VMEM(shape, kind) for shape, kind in shapes),
        in_specs=[any_spec] * 8,
        out_specs=(any_spec,) * 5,
        scratch_shapes=[pltpu.VMEM(shape, kind) for shape, kind in scratch]
        + [
            pltpu.SemaphoreType.DMA((5,)),
            pltpu.SemaphoreType.DMA((len(GROUPS),)),
            pltpu.SemaphoreType.DMA((len(GROUPS),)),
        ],
        compiler_params=pltpu.CompilerParams(
            collective_id=0, has_side_effects=True, vmem_limit_bytes=40 << 20
        ),
        name="video_block_backward",
    )(*[pltpu.with_memory_space_constraint(a, pltpu.HBM) for a in operands])
    outs = pl.pallas_call(
        write_out,
        out_shape=tuple(jax.ShapeDtypeStruct(shape, kind) for shape, kind in shapes),
        in_specs=[any_spec] * 5,
        out_specs=(any_spec,) * 5,
        scratch_shapes=[pltpu.SemaphoreType.DMA((5,))],
        compiler_params=pltpu.CompilerParams(vmem_limit_bytes=1 << 20),
        name="write_out",
    )(*outs)
    return (outs[0].reshape(1, 1, COLS, CH), outs[1].reshape(1, HEAD, CH), outs[2], outs[3], outs[4])


def solution(mesh):
    return jax.shard_map(
        body,
        mesh=mesh,
        in_specs=(
            P("frame", "row", None, None),
            P("row", "frame", None),
            P("frame", "row", None, None),
            P("row", "frame", None),
            P(),
            P(),
            P(),
            P(),
        ),
        out_specs=(
            P("frame", "row", None, None),
            P("row", "frame", None),
            P(None, "row", None),
            P(None, "row", None),
            P(None, "row"),
        ),
        check_vma=False,
    )
```

```python
import functools
import math

import jax
import jax.numpy as jnp
from jax import lax
from jax.experimental import pallas as pl
from jax.experimental.pallas import tpu as pltpu
from jax.sharding import PartitionSpec as P

MESH = pl.DeviceIdType.MESH
F32 = jnp.float32
BF16 = jnp.bfloat16
COLS = 128
CH = 256
HEAD = 8
OWN = 64
FIRST = COLS + HEAD
ROWS = 224
NX, NY, NZ, NF, NR = 4, 8, 8, 16, 32
AROUND_X = (2, 1, 3)
AROUND_8 = (4, 3, 5, 2, 6, 1, 7)
SCALE = 1.0 / math.sqrt(17 * 32 * 128)


GROUPS = (
    "vrow0", "vrow1", "cnext", "hv0", "hv1", "hv2", "hb0", "hb1", "hb2", "chg", "prow0", "prow1", "phr0", "phr1",
    "phb0", "phb1", "phb2", "gh", "lsib", "csib", "psib", "total",
    "x0", "x1", "z0", "z1", "zf", "xl", "y0", "y1", "y2", "vz", "vx", "vy",
)
SEM = {name: i for i, name in enumerate(GROUPS)}


def stacked(piece):
    half = CH // 2
    return jnp.concatenate([piece[..., :half], piece[..., half:]], axis=-2).astype(BF16)


def unstacked(piece):
    rows = piece.astype(F32)
    return jnp.concatenate([rows[:HEAD], rows[HEAD:]], axis=1)


def dot(a, b):
    return jnp.dot(a, b, preferred_element_type=F32)


def dot_back(a, b):
    return lax.dot_general(a, b, (((1,), (1,)), ((), ())), preferred_element_type=F32)


def dot_outer(a, b):
    return lax.dot_general(a, b, (((0,), (0,)), ((), ())), preferred_element_type=F32)


def down(v):
    return pltpu.roll(v, 1, 0)


def up(v):
    return pltpu.roll(v, v.shape[0] - 1, 0)


def kernel(
    vid_h, vh_h, cot_h, ch_h, mod_h, cw_h, cb_h, tw_h,
    gt_o, gh_o, taps_o, gv_o,
    vc, heads, vecs, wv, tw, gt_v, gh_v, gv_v,
    vhs, chs, vrow, cnext, hv, chg,
    left, lsib, right, back, prow, pgt, pgh, pgb, phr, phb, ghs, ghr, wsel,
    prod, g, xb, h, zb, gz, zfb, hx, xlb, yb, total,
    vec, vzb, vxb, vyb,
    lsem, ss, rs, known,
):
    f = lax.axis_index("frame")
    r = lax.axis_index("row")
    y, c = lax.div(f, 2), lax.rem(f, 2)
    x, z = lax.div(r, NZ), lax.rem(r, NZ)

    def at(fo, ro):
        return (lax.rem(f + fo + NF, NF), lax.rem(r + ro + NR, NR))

    def at_x(o):
        return (f, lax.rem(x + o, NX) * NZ + z)

    def at_z(o):
        return (f, x * NZ + lax.rem(z + o, NZ))

    def at_y(o):
        return (lax.rem(y + o, NY) * 2 + c, r)

    sibling = (y * 2 + 1 - c, r)
    low, high = f == 0, f == NF - 1
    owner = low | high
    middle = (f == NF // 2 - 1) | (f == NF // 2)
    mine_at = jnp.where(f < NF // 2, 0, NF - 1)
    place = lax.rem(f, NF // 2)

    def remote(src, dst, sem, device, recv=None):
        return pltpu.make_async_remote_copy(
            src_ref=src, dst_ref=dst, send_sem=ss.at[sem], recv_sem=rs.at[sem if recv is None else recv],
            device_id=device, device_id_type=MESH,
        )

    sent = {}

    def send(src, dst, name, device, whole):
        remote(src, dst, SEM[name], device).start()
        sent[name] = whole

    def arrived(name):
        whole = sent[name]
        remote(whole, whole, SEM[name], sibling).wait_recv()

    barrier = pltpu.get_barrier_semaphore()

    def row_ok(ro):
        return (r + ro >= 0) & (r + ro < NR)

    def greet(device, semaphore=barrier):
        pl.semaphore_signal(semaphore, inc=1, device_id=device, device_id_type=MESH)

    rows_beside = jnp.where(row_ok(-1), 1, 0) + jnp.where(row_ok(1), 1, 0)
    for ro in (-1, 1):

        @pl.when(row_ok(ro))
        def _():
            greet(at(0, ro))

    greet(sibling)
    greet(at(1, 0))
    greet(at(2, 0))
    ring = [at_x(1), at_x(NX - 1), at_z(1), at_z(NZ - 1), at_y(1), at_y(NY - 1)]
    for device in ring:
        greet(device)
    for ro in (-1, 0, 1):

        @pl.when(owner & row_ok(ro))
        def _():
            for o in range(0 if ro else 1, NF // 2 + 1):
                greet((jnp.where(low, o, NF - 1 - o), at(0, ro)[1]))
            greet((NF - 1 - f, at(0, ro)[1]))

    greeted = 9 + 2 * rows_beside + jnp.where(f != mine_at, 1, 0) + jnp.where(middle | owner, rows_beside + 1, 0)

    def local(group, src, dst):
        return pltpu.make_async_copy(src, dst, lsem.at[group])

    for group, src, dst in (
        (0, vid_h, vc.at[0]), (0, cot_h, vc.at[1]), (1, vh_h, heads.at[0]), (1, ch_h, heads.at[1]),
        (2, mod_h, vecs.at[0]), (2, cb_h, vecs.at[1]),
        (3, cw_h.at[:, 0], wv.at[0]), (3, cw_h.at[:, 1], wv.at[1]), (3, cw_h.at[:, 2], wv.at[2]),
        (4, tw_h, tw),
    ):
        local(group, src, dst).start()
    pl.semaphore_wait(barrier, greeted)
    for device in ring:
        greet(device, known.at[0])

    def head_piece(to, slot, ro, sem):
        return remote(
            vhs, hv.at[10 * (1 - ro) + slot], SEM[sem] + 1 - ro, (to, at(0, ro)[1]), SEM["hv0"] + 1 - ro
        )

    def own_piece(ro):
        return head_piece(mine_at, place + 1, ro, "hv0")

    def edge_piece(ro):
        return head_piece(NF - 1 - mine_at, jnp.where(f < NF // 2, 0, 9), ro, "hb0")

    def head_cot():
        return remote(chs, chg.at[place], SEM["chg"], (mine_at, r))

    def to_row(src, dst, name, ro):
        i = (1 - ro) // 2
        return remote(src, dst.at[i], SEM[name] + i, at(0, ro))

    def from_row(dst, name, dr):
        i = (1 + dr) // 2

        @pl.when(row_ok(dr))
        def _():
            remote(dst.at[i], dst.at[i], SEM[name] + i, sibling).wait_recv()

    for ro in (-1, 1):

        @pl.when(row_ok(ro))
        def _():
            to_row(vid_h, vrow, "vrow0", ro).start()

    send(cot_h, cnext.at[0], "cnext", at(-1, 0), cnext)
    send(cot_h, cnext.at[1], "cnext", at(-2, 0), cnext)

    for group, whole in ((1, heads), (0, vc), (2, vecs)):
        local(group, whole, whole).wait()
    vid, cot = vc.at[0], vc.at[1]
    vh32, ch32 = heads[0].astype(F32), heads[1].astype(F32)
    vhs[...] = stacked(vh32)
    chs[...] = stacked(ch32)
    left[COLS:ROWS, 0 : 3 * CH] = jnp.zeros((ROWS - COLS, 3 * CH), BF16)
    right[1, 0, COLS:ROWS, :] = jnp.zeros((ROWS - COLS, 3 * CH), BF16)
    back[:, COLS:ROWS, :] = jnp.zeros((3, ROWS - COLS, CH), BF16)
    for ro in (-1, 0, 1):

        @pl.when(row_ok(ro) if ro else f != mine_at)
        def _():
            own_piece(ro).start()

        @pl.when(middle & row_ok(ro))
        def _():
            edge_piece(ro).start()

    @pl.when(f != mine_at)
    def _():
        head_cot().start()

    @pl.when(owner)
    def _():
        hv[10 + place + 1] = vhs[...]
        chg[place] = chs[...]

    row_ids = lax.broadcasted_iota(jnp.int32, (HEAD, CH), 0)
    zero8 = jnp.zeros((HEAD, CH), F32)
    zero16 = jnp.zeros((2 * HEAD, CH), F32)
    modv = vecs[0]

    def joined(buffer, first):
        return jnp.concatenate([unstacked(buffer[first + k]) for k in range(OWN // HEAD)], axis=0)

    def head_block(before, own, after):
        before = jnp.where((row_ids == HEAD - 1) & high, unstacked(before), 0.0)
        after = jnp.where((row_ids == 0) & low, unstacked(after), 0.0)
        return jnp.concatenate([before, own, after, zero16], axis=0)

    local(4, tw, tw).wait()
    arrived("cnext")

    @pl.when(owner)
    def _():
        whole = chg.at[pl.ds(0, NF // 2 - 1)]
        remote(whole, whole, SEM["chg"], sibling).wait_recv()
        heads_of = (
            joined(chg, 0),
            jnp.where(low, cot[0:OWN].astype(F32), cnext[0, OWN:COLS].astype(F32)),
            jnp.where(low, cnext[0, 0:OWN].astype(F32), cnext[1, OWN:COLS].astype(F32)),
        )
        for k in range(3):
            block = jnp.concatenate([zero8, heads_of[k], zero8, zero16], axis=0)
            right[1, 0, COLS:ROWS, k * CH : (k + 1) * CH] = block.astype(BF16)

    grad = None
    for k in range(3):
        tail = cot[...]
        if k > 0:
            tail = jnp.where(f + k < NF, cnext[k - 1].astype(F32), 0.0).astype(BF16)
        right[1, 0, 0:COLS, k * CH : (k + 1) * CH] = tail
        term = dot_back(right[1, 0, :, k * CH : (k + 1) * CH], tw[k])
        grad = term if grad is None else grad + term
    send(right.at[1, 0], right.at[1, 1], "csib", sibling, right.at[1, 1])

    for dr in (-1, 1):
        from_row(vrow, "vrow0", dr)
    for p in range(3):
        dr = p - 1
        rows = (vid[...] if dr == 0 else vrow[0 if dr < 0 else 1]).astype(F32)
        if dr != 0:
            rows = jnp.where(row_ok(dr), rows, 0.0)
        left[0:COLS, p * CH : (p + 1) * CH] = (rows * modv).astype(BF16)

    @pl.when(owner)
    def _():
        for p in range(3):
            dr = p - 1
            pieces = hv.at[pl.ds(0, 9 if dr else 8)]

            @pl.when(row_ok(dr))
            def _():
                remote(pieces, pieces, SEM["hv0"] + p, sibling).wait_recv()

            block = head_block(hv[10 * p], joined(hv, 10 * p + 1), hv[10 * p + 9])
            if dr != 0:
                block = jnp.where(row_ok(dr), block, 0.0)
            left[COLS:ROWS, p * CH : (p + 1) * CH] = (block * modv).astype(BF16)

    pl.semaphore_wait(known.at[0], len(ring))
    further = [at_z(2), at_z(NZ - 2), at_y(2), at_y(NY - 2)]
    for device in further:
        greet(device, known.at[1])

    local(3, wv, wv).wait()

    xs = left[:, 0 : 3 * CH]
    pre = down(dot(xs, wv[0].reshape(3 * CH, CH)))
    pre = pre + dot(xs, wv[1].reshape(3 * CH, CH))
    pre = pre + up(dot(xs, wv[2].reshape(3 * CH, CH)))
    pre = pre + vecs[1]
    sig = jax.nn.sigmoid(pre)
    left[:, 3 * CH : 4 * CH] = (pre * sig).astype(BF16)
    slope = sig * (1.0 + pre * (1.0 - sig))

    half_other = pl.multiple_of(2 * CH * (1 - c), 2 * CH)
    half_mine = pl.multiple_of(2 * CH * c, 2 * CH)
    send(left.at[:, pl.ds(half_other, 2 * CH)], lsib.at[1], "lsib", sibling, lsib.at[1])

    pg16 = (grad.astype(BF16).astype(F32) * slope).astype(BF16)
    pg = pg16.astype(F32)
    right[0, 0, :, CH : 2 * CH] = pg16
    theirs = right.at[0, 1, :, pl.ds(CH, CH)]
    send(right.at[0, 0, :, pl.ds(CH, CH)], theirs, "psib", sibling, theirs)
    pgt[...] = pg16[0:COLS]
    pg_own = pg[FIRST : FIRST + OWN]
    pgh[...] = pg_own.astype(BF16)
    pgb[...] = stacked(jnp.where(low, pg_own[OWN - HEAD :], pg_own[:HEAD]))

    def head_rows(ro):
        return to_row(pgh, phr, "phr0", ro)

    def head_edge(ro):
        return remote(pgb, phb.at[1 - ro], SEM["phb0"] + 1 - ro, (NF - 1 - f, at(0, ro)[1]))

    for ro in (-1, 1):

        @pl.when(row_ok(ro))
        def _():
            to_row(pgt, prow, "prow0", ro).start()

        @pl.when(owner & row_ok(ro))
        def _():
            head_rows(ro).start()

    for ro in (-1, 0, 1):

        @pl.when(owner & row_ok(ro))
        def _():
            head_edge(ro).start()

    right[0, 0, :, 0:CH] = up(pg).astype(BF16)
    right[0, 0, :, 2 * CH : 3 * CH] = down(pg).astype(BF16)
    bias_terms = jnp.sum(pg, axis=0, keepdims=True)
    vec[0] = jnp.concatenate([bias_terms[:, 0:128], bias_terms[:, 128:256], jnp.zeros((2, 128), F32)], axis=0)

    lsib[0] = left[:, pl.ds(half_mine, 2 * CH)]

    def terms(j, core):
        return dot_outer(lsib[core, :, j * CH : (j + 1) * CH], right[0 if j == 0 else c, core])

    for j in range(2):
        prod[j] = terms(j, 0)
    arrived("lsib")
    arrived("csib")
    arrived("psib")
    other = right[0, 1, :, CH : 2 * CH].astype(F32)
    right[0, 1, :, 0:CH] = up(other).astype(BF16)
    right[0, 1, :, 2 * CH : 3 * CH] = down(other).astype(BF16)

    def pair_of_taps(t):
        parts = [
            prod[tap // 3, :, (tap % 3) * CH : (tap % 3 + 1) * CH].reshape(NX, NZ, 8, CH)
            for tap in (2 * t, 2 * t + 1)
        ]
        return jnp.concatenate(parts, axis=2).astype(BF16)

    pl.semaphore_wait(known.at[1], len(further))
    for o in AROUND_X:
        send(vec.at[0], vxb.at[o - 1], "vx", at_x(o), vxb)
    for j in range(2):
        prod[j] = prod[j] + terms(j, 1)
        for t in (0,) if j == 0 else (1,):
            g[t] = pair_of_taps(t)
            for o in AROUND_X:
                to = lax.rem(x + o, NX)
                send(g.at[t, to], xb.at[t, o - 1], f"x{t}", at_x(o), xb.at[t])
    block = pair_of_taps(2)
    for i in range(NX):
        gz[:, i] = block[i]
    for o in AROUND_8:
        send(gz.at[lax.rem(z + o, NZ)], zfb.at[o - 1], "zf", at_z(o), zfb)

    def weight_rows(tap):
        both = wv[tap % 3, tap // 3, pl.ds(pl.multiple_of(16 * lax.div(r, 2), 16), 16), :].astype(F32)
        return jnp.where(lax.rem(r, 2) == 0, both[:8], both[8:])

    for i in range(6):
        wsel[i] = jnp.where(c == 0, weight_rows(i), weight_rows(6 + i) if i < 3 else 0.0)

    for dr in (-1, 1):
        from_row(prow, "prow0", dr)
    for p in range(3):
        dr = 1 - p
        if dr == 0:
            rows = pgt[...]
        else:
            rows = prow[0 if dr < 0 else 1].astype(F32)
            rows = jnp.where(row_ok(dr), rows, 0.0).astype(BF16)
        back[p, 0:COLS, :] = rows

    @pl.when(owner)
    def _():
        for dr in (-1, 1):
            from_row(phr, "phr0", dr)
        for p in range(3):
            dr = 1 - p
            edge = phb.at[dr + 1]

            @pl.when(row_ok(dr))
            def _():
                remote(edge, edge, SEM["phb0"] + dr + 1, sibling).wait_recv()

            own = pg_own if dr == 0 else phr[0 if dr < 0 else 1].astype(F32)
            block = head_block(phb[dr + 1], own, phb[dr + 1])
            if dr != 0:
                block = jnp.where(row_ok(dr), block, 0.0)
            back[p, COLS:ROWS, :] = block.astype(BF16)

    convs = []
    for q in range(3):
        acc = None
        for p in range(3):
            term = dot_back(back[p], wv[q, p])
            acc = term if acc is None else acc + term
        convs.append(acc)
    mod_grad = up(convs[0]) + convs[1] + down(convs[2])
    tail_grad = mod_grad[0:COLS]
    head_grad = mod_grad[FIRST : FIRST + OWN]
    gt_v[...] = (cot[...].astype(F32) + modv * tail_grad).astype(BF16)

    def head_result(o):
        to = jnp.where(low, o, NF - 1 - o)
        return remote(ghs.at[lax.rem(to, NF // 2)], ghr, SEM["gh"], (to, r))

    @pl.when(owner)
    def _():
        result = joined(chg, 0) + modv * head_grad
        for k in range(OWN // HEAD):
            ghs[k] = stacked(result[k * HEAD : (k + 1) * HEAD])
        for o in range(1, NF // 2):
            head_result(o).start()
        ghr[...] = ghs[place]

    local(0, gt_v, gt_o).start()
    def total_of(own, parts, count):
        acc = own.astype(F32)
        for i in range(count):
            acc = acc + parts[i].astype(F32)
        return acc

    products = []

    def over_y(t, own):
        products.append(own[0:8] * wsel[2 * t] + own[8:16] * wsel[2 * t + 1])
        yb[y, t] = own.astype(BF16)
        for o in AROUND_8:
            send(yb.at[y, t], yb.at[y, t], f"y{t}", at_y(o), yb.at[pl.ds(0, NY - 1), t])

    arrived("vx")
    vec[1] = total_of(vec[0], vxb, NX - 1)
    for o in AROUND_8:
        send(vec.at[1], vzb.at[o - 1], "vz", at_z(o), vzb)
    for t in range(2):
        arrived(f"x{t}")
        h[t] = total_of(g[t, x], xb.at[t], NX - 1).astype(BF16)
        for o in AROUND_8:
            send(h.at[t, lax.rem(z + o, NZ)], zb.at[t, o - 1], f"z{t}", at_z(o), zb.at[t])
    arrived("zf")
    hx[...] = total_of(gz[z], zfb, NZ - 1).astype(BF16)
    for o in AROUND_X:
        send(hx.at[lax.rem(x + o, NX)], xlb.at[o - 1], "xl", at_x(o), xlb)
    arrived("z0")
    over_y(0, total_of(h[0, z], zb.at[0], NZ - 1))
    arrived("xl")
    over_y(2, total_of(hx[x], xlb, NX - 1))
    arrived("z1")
    over_y(1, total_of(h[1, z], zb.at[1], NZ - 1))
    arrived("vz")
    per_row = products[0] + products[1] + products[2]
    per_row = jnp.sum(per_row, axis=1, keepdims=True)
    lanes = lax.broadcasted_iota(jnp.int32, (8, 128), 1)
    in_lanes = jnp.where(lanes == lax.broadcasted_iota(jnp.int32, (8, 128), 0), per_row, 0.0)
    scale_terms = jnp.sum(in_lanes, axis=0, keepdims=True)
    summed = total_of(vec[1], vzb, NZ - 1)
    vyb[f] = jnp.concatenate([summed[0:2], scale_terms, jnp.zeros((1, 128), F32)], axis=0)
    for o in AROUND_8:
        for core in (c, 1 - c):
            send(vyb.at[f], vyb.at[f], "vy", (lax.rem(y + o, NY) * 2 + core, r), vyb.at[pl.ds(0, NF - 1)])
    send(vyb.at[f], vyb.at[f], "vy", sibling, vyb.at[pl.ds(0, NF - 1)])
    arrived("vy")
    both = total_of(vyb[0], vyb.at[pl.ds(1, NF - 1)], NF - 1) * SCALE
    lower = r < NR // 2
    two = jnp.concatenate(
        [
            jnp.where(lower, both[0:1], both[1:2]),
            jnp.where(lower, modv[:, 0:128], modv[:, 128:256]),
            jnp.zeros((6, 128), F32),
        ],
        axis=0,
    )
    turned = pltpu.roll(two, lax.rem(128 - 8 * lax.rem(r, 16), 128), 1)
    gv_v[...] = jnp.concatenate([both[2:3, 0:8] / turned[1:2, 0:8], turned[0:1, 0:8]], axis=0)
    local(2, gv_v, gv_o).start()

    @pl.when(f != mine_at)
    def _():
        remote(ghr, ghr, SEM["gh"], sibling).wait_recv()

    gh_v[...] = unstacked(ghr[...]).astype(BF16)
    local(1, gh_v, gh_o).start()
    for name in ("y0", "y2", "y1"):
        arrived(name)
    acc = total_of(yb[0], yb.at[pl.ds(1, NY - 1)], NY - 1)
    total[...] = (acc * SCALE).reshape(6, 8, CH)
    send(total, taps_o.at[pl.ds(6 * c, 6)], "total", sibling, total)
    local(3, total, taps_o.at[pl.ds(6 * c, 6)]).start()
    arrived("total")
    for name, whole in sent.items():
        remote(whole, whole, SEM[name], sibling).wait_send()

    for ro in (-1, 0, 1):

        @pl.when(row_ok(ro) if ro else f != mine_at)
        def _():
            own_piece(ro).wait_send()

        @pl.when(middle & row_ok(ro))
        def _():
            edge_piece(ro).wait_send()

        @pl.when(owner & row_ok(ro))
        def _():
            head_edge(ro).wait_send()
            if ro:
                head_rows(ro).wait_send()

        if ro:

            @pl.when(row_ok(ro))
            def _():
                to_row(vid, vrow, "vrow0", ro).wait_send()
                to_row(pgt, prow, "prow0", ro).wait_send()

    @pl.when(f != mine_at)
    def _():
        head_cot().wait_send()

    @pl.when(owner)
    def _():
        whole = ghs.at[pl.ds(0, NF // 2 - 1)]
        remote(whole, whole, SEM["gh"], sibling).wait_send()

    for i, whole in enumerate((gt_v, gh_v, gv_v, total)):
        local(i, whole, whole).wait()


def write_out(gt, gh, taps, gv, gt_o, gh_o, gc_o, gtw_o, gv_o, sems):
    pairs = ((gt, gt_o), (gh, gh_o), (taps.at[pl.ds(0, 9)], gc_o), (taps.at[pl.ds(9, 3)], gtw_o), (gv, gv_o))
    copies = [pltpu.make_async_copy(src, dst, sems.at[i]) for i, (src, dst) in enumerate(pairs)]
    for copy in copies:
        copy.start()
    for copy in copies:
        copy.wait()


def body(video_tail, video_head, cotangent_tail, cotangent_head, modulation, conv_weight, conv_bias, temporal_weight):
    any_spec = pl.BlockSpec(memory_space=pl.ANY)
    scratch = [
        ((2, COLS, CH), BF16), ((2, HEAD, CH), BF16), ((2, 1, CH), F32),
        ((3, 3, CH, CH), BF16), ((3, CH, CH), BF16),
        ((COLS, CH), BF16), ((HEAD, CH), BF16), ((2, 8), F32),
        ((16, 128), BF16), ((16, 128), BF16), ((2, COLS, CH), BF16), ((2, COLS, CH), BF16),
        ((30, 16, 128), BF16), ((NF // 2, 16, 128), BF16),
        ((ROWS, 4 * CH), BF16), ((2, ROWS, 2 * CH), BF16), ((2, 2, ROWS, 3 * CH), BF16),
        ((3, ROWS, CH), BF16), ((2, COLS, CH), BF16), ((COLS, CH), BF16), ((OWN, CH), BF16),
        ((16, 128), BF16), ((2, OWN, CH), BF16), ((3, 16, 128), BF16), ((NF // 2, 16, 128), BF16),
        ((16, 128), BF16), ((6, 8, CH), F32),
        ((2, CH, 3 * CH), F32), ((2, NX, NZ, 16, CH), BF16), ((2, NX - 1, NZ, 16, CH), BF16),
        ((2, NZ, 16, CH), BF16), ((2, NZ - 1, 16, CH), BF16),
        ((NZ, NX, 16, CH), BF16), ((NZ - 1, NX, 16, CH), BF16), ((NX, 16, CH), BF16),
        ((NX - 1, 16, CH), BF16), ((NY, 3, 16, CH), BF16),
        ((6, 8, CH), F32),
        ((2, 4, 128), F32), ((NZ - 1, 4, 128), F32), ((NX - 1, 4, 128), F32), ((NF, 4, 128), F32),
    ]
    shapes = [((COLS, CH), BF16), ((HEAD, CH), BF16), ((9, 8, CH), F32), ((3, 8, CH), F32), ((2, 8), F32)]
    operands = [
        video_tail.reshape(COLS, CH),
        video_head.reshape(HEAD, CH),
        cotangent_tail.reshape(COLS, CH),
        cotangent_head.reshape(HEAD, CH),
        modulation.reshape(1, CH),
        conv_weight.reshape(3, 3, CH, CH),
        conv_bias.reshape(1, CH),
        temporal_weight,
    ]
    outs = pl.pallas_call(
        kernel,
        out_shape=tuple(pltpu.VMEM(shape, kind) for shape, kind in shapes[:2] + [((12, 8, CH), F32), shapes[4]]),
        in_specs=[any_spec] * 8,
        out_specs=(any_spec,) * 4,
        scratch_shapes=[pltpu.VMEM(shape, kind) for shape, kind in scratch]
        + [
            pltpu.SemaphoreType.DMA((5,)),
            pltpu.SemaphoreType.DMA((len(GROUPS),)),
            pltpu.SemaphoreType.DMA((len(GROUPS),)),
            pltpu.SemaphoreType.REGULAR((2,)),
        ],
        compiler_params=pltpu.CompilerParams(
            collective_id=0, has_side_effects=True, vmem_limit_bytes=40 << 20
        ),
        name="video_block_backward",
    )(*[pltpu.with_memory_space_constraint(a, pltpu.HBM) for a in operands])
    outs = pl.pallas_call(
        write_out,
        out_shape=tuple(jax.ShapeDtypeStruct(shape, kind) for shape, kind in shapes),
        in_specs=[any_spec] * 4,
        out_specs=(any_spec,) * 5,
        scratch_shapes=[pltpu.SemaphoreType.DMA((5,))],
        compiler_params=pltpu.CompilerParams(vmem_limit_bytes=1 << 20),
        name="write_out",
    )(*outs)
    return (outs[0].reshape(1, 1, COLS, CH), outs[1].reshape(1, HEAD, CH), outs[2], outs[3], outs[4])


def solution(mesh):
    return jax.shard_map(
        body,
        mesh=mesh,
        in_specs=(
            P("frame", "row", None, None),
            P("row", "frame", None),
            P("frame", "row", None, None),
            P("row", "frame", None),
            P(),
            P(),
            P(),
            P(),
        ),
        out_specs=(
            P("frame", "row", None, None),
            P("row", "frame", None),
            P(None, "row", None),
            P(None, "row", None),
            P(None, "row"),
        ),
        check_vma=False,
    )
```

```python
import functools
import math

import jax
import jax.numpy as jnp
from jax import lax
from jax.experimental import pallas as pl
from jax.experimental.pallas import tpu as pltpu
from jax.sharding import PartitionSpec as P

MESH = pl.DeviceIdType.MESH
F32 = jnp.float32
BF16 = jnp.bfloat16
COLS = 128
CH = 256
HEAD = 8
OWN = 64
FIRST = COLS + HEAD
ROWS = 224
NX, NY, NZ, NF, NR = 4, 8, 8, 16, 32
AROUND_X = (2, 1, 3)
AROUND_8 = (4, 3, 5, 2, 6, 1, 7)
HALVES = (slice(0, CH // 2), slice(CH // 2, CH))
SCALE = 1.0 / math.sqrt(17 * 32 * 128)


ARRIVE = (
    "vrow0", "vrow1", "cnext", "hv0", "hv1", "hv2", "chg", "prow0", "prow1", "ph0", "ph1", "ph2", "gh",
    "sib", "psib", "total", "x0", "x1", "x2", "x3", "z0", "z1", "z2", "z3", "last1", "last2", "ends", "y", "vz", "vx", "vy",
)
LEAVE = ("all", "up", "same", "down", "ph0", "ph1", "ph2", "vec", "odd")
UNITS = 448
RECV = {name: i for i, name in enumerate(ARRIVE)}
SENT = {name: i for i, name in enumerate(LEAVE)}


def stacked(piece):
    half = CH // 2
    return jnp.concatenate([piece[..., :half], piece[..., half:]], axis=-2).astype(BF16)


def unstacked(piece):
    rows = piece.astype(F32)
    return jnp.concatenate([rows[:HEAD], rows[HEAD:]], axis=1)


def dot(a, b):
    return jnp.dot(a, b, preferred_element_type=F32)


def dot_back(a, b):
    return lax.dot_general(a, b, (((1,), (1,)), ((), ())), preferred_element_type=F32)


def dot_outer(a, b):
    return lax.dot_general(a, b, (((0,), (0,)), ((), ())), preferred_element_type=F32)


def down(v):
    return pltpu.roll(v, 1, 0)


def up(v):
    return pltpu.roll(v, v.shape[0] - 1, 0)


def kernel(
    vid_h, vh_h, cot_h, ch_h, mod_h, cw_h, cb_h, tw_h,
    gt_o, gh_o, taps_o, gv_o,
    vc, heads, vecs, wv, tw, gt_v, gh_v, gv_v,
    vhs, chs, vrow, cnext, hv, chg,
    left, lsib, right, back, prow, pgt, pgh, pgb, phr, phb, ghs, ghr, wsel,
    prod, g, xb, h, zb, gz, zfb, hx, xlb, gy, yfb, hy, rows_in, ends, psum, yb, total,
    vec, vzb, vxb, vyb,
    sizes, lsem, ss, rs, known,
):
    f = lax.axis_index("frame")
    r = lax.axis_index("row")
    y, c = lax.div(f, 2), lax.rem(f, 2)
    x, z = lax.div(r, NZ), lax.rem(r, NZ)

    def at(fo, ro):
        return (lax.rem(f + fo + NF, NF), lax.rem(r + ro + NR, NR))

    def at_x(o):
        return (f, lax.rem(x + o, NX) * NZ + z)

    def at_z(o):
        return (f, x * NZ + lax.rem(z + o, NZ))

    def at_y(o):
        return (lax.rem(y + o, NY) * 2 + c, r)

    sibling = (y * 2 + 1 - c, r)
    low, high = f == 0, f == NF - 1
    owner = low | high
    middle = (f == NF // 2 - 1) | (f == NF // 2)
    mine_at = jnp.where(f < NF // 2, 0, NF - 1)
    place = lax.rem(f, NF // 2)

    def remote(src, dst, leave, arrive, device):
        return pltpu.make_async_remote_copy(
            src_ref=src, dst_ref=dst, send_sem=ss.at[leave], recv_sem=rs.at[arrive],
            device_id=device, device_id_type=MESH,
        )

    on_both, on_0, on_1 = [], [], []

    def send(src, dst, name, device, leave="all", tally=on_both):
        remote(src, dst, SENT[leave], RECV[name], device).start()
        if leave == "all":
            tally.append(math.prod(src.shape) * src.dtype.itemsize // 4096)

    def wait_arrived(name, whole, more=0):
        remote(whole, whole, 0, RECV[name] + more, sibling).wait_recv()

    def wait_left(name, count, more=0):
        whole = sizes.at[pl.ds(0, count)]
        remote(whole, whole, SENT[name] + more, 0, sibling).wait_send()

    barrier = pltpu.get_barrier_semaphore()

    def row_ok(ro):
        return (r + ro >= 0) & (r + ro < NR)

    def greet(device, semaphore=barrier):
        pl.semaphore_signal(semaphore, inc=1, device_id=device, device_id_type=MESH)

    rows_beside = jnp.where(row_ok(-1), 1, 0) + jnp.where(row_ok(1), 1, 0)
    for ro in (-1, 1):

        @pl.when(row_ok(ro))
        def _():
            greet(at(0, ro))

    greet(sibling)
    greet(at(1, 0))
    greet(at(2, 0))
    ring = [at_x(1), at_x(NX - 1), at_z(1), at_z(NZ - 1), at_y(1), at_y(NY - 1)]
    for device in ring:
        greet(device)
    for ro in (-1, 0, 1):

        @pl.when(owner & row_ok(ro))
        def _():
            for o in range(0 if ro else 1, NF // 2 + 1):
                greet((jnp.where(low, o, NF - 1 - o), at(0, ro)[1]))
            greet((NF - 1 - f, at(0, ro)[1]))

    greeted = 9 + 2 * rows_beside + jnp.where(f != mine_at, 1, 0) + jnp.where(middle | owner, rows_beside + 1, 0)

    def local(group, src, dst):
        return pltpu.make_async_copy(src, dst, lsem.at[group])

    for group, src, dst in (
        (0, vid_h, vc.at[0]), (0, cot_h, vc.at[1]), (1, vh_h, heads.at[0]), (1, ch_h, heads.at[1]),
        (2, mod_h, vecs.at[0]), (2, cb_h, vecs.at[1]),
        (3, cw_h.at[:, 0], wv.at[0]), (3, cw_h.at[:, 1], wv.at[1]), (3, cw_h.at[:, 2], wv.at[2]),
        (4, tw_h, tw),
    ):
        local(group, src, dst).start()
    for group, whole in ((1, heads), (2, vecs), (0, vc)):
        local(group, whole, whole).wait()
    vid, cot = vc.at[0], vc.at[1]
    vh32, ch32 = heads[0].astype(F32), heads[1].astype(F32)
    vhs[...] = stacked(vh32)
    chs[...] = stacked(ch32)
    left[COLS:ROWS, 0 : 3 * CH] = jnp.zeros((ROWS - COLS, 3 * CH), BF16)
    right[1, 0, COLS:ROWS, :] = jnp.zeros((ROWS - COLS, 3 * CH), BF16)
    back[:, COLS:ROWS, :] = jnp.zeros((3, ROWS - COLS, CH), BF16)
    pl.semaphore_wait(barrier, greeted)
    for device in ring:
        greet(device, known.at[0])

    def head_piece(to, slot, ro, leave):
        return remote(
            vhs, hv.at[10 * (1 - ro) + slot], SENT[leave] + 1 + ro, RECV["hv0"] + 1 - ro, (to, at(0, ro)[1])
        )

    def own_piece(ro):
        return head_piece(mine_at, place + 1, ro, "up")

    def edge_piece(ro):
        return head_piece(NF - 1 - mine_at, jnp.where(f < NF // 2, 0, 9), ro, "ph0")

    def head_cot():
        return remote(chs, chg.at[place], SENT["same"], RECV["chg"], (mine_at, r))

    def to_row(src, dst, name, ro, leave="up"):
        i = (1 - ro) // 2
        return remote(src, dst.at[i], SENT[leave] + 1 + ro, RECV[name] + i, at(0, ro))

    def from_row(dst, name, dr):
        i = (1 + dr) // 2

        @pl.when(row_ok(dr))
        def _():
            wait_arrived(name, dst.at[i], i)

    for ro in (-1, 0, 1):

        @pl.when(row_ok(ro) if ro else f != mine_at)
        def _():
            own_piece(ro).start()

        @pl.when(middle & row_ok(ro))
        def _():
            edge_piece(ro).start()

    @pl.when(f != mine_at)
    def _():
        head_cot().start()

    @pl.when(owner)
    def _():
        hv[10 + place + 1] = vhs[...]
        chg[place] = chs[...]

    for ro in (-1, 1):

        @pl.when(row_ok(ro))
        def _():
            to_row(vid, vrow, "vrow0", ro).start()

    send(cot, cnext.at[0], "cnext", at(-1, 0))
    send(cot, cnext.at[1], "cnext", at(-2, 0))

    row_ids = lax.broadcasted_iota(jnp.int32, (HEAD, CH), 0)
    zero8 = jnp.zeros((HEAD, CH), F32)
    zero16 = jnp.zeros((2 * HEAD, CH), F32)
    modv = vecs[0]

    def joined(buffer, first):
        return jnp.concatenate([unstacked(buffer[first + k]) for k in range(OWN // HEAD)], axis=0)

    def head_block(before, own, after):
        before = jnp.where((row_ids == HEAD - 1) & high, unstacked(before), 0.0)
        after = jnp.where((row_ids == 0) & low, unstacked(after), 0.0)
        return jnp.concatenate([before, own, after, zero16], axis=0)

    local(4, tw, tw).wait()
    wait_arrived("cnext", cnext)

    @pl.when(owner)
    def _():
        wait_arrived("chg", chg.at[pl.ds(0, NF // 2 - 1)])
        heads_of = (
            joined(chg, 0),
            jnp.where(low, cot[0:OWN].astype(F32), cnext[0, OWN:COLS].astype(F32)),
            jnp.where(low, cnext[0, 0:OWN].astype(F32), cnext[1, OWN:COLS].astype(F32)),
        )
        for k in range(3):
            block = jnp.concatenate([zero8, heads_of[k], zero8, zero16], axis=0)
            right[1, 0, COLS:ROWS, k * CH : (k + 1) * CH] = block.astype(BF16)

    grad = None
    for k in range(3):
        tail = cot[...]
        if k > 0:
            tail = jnp.where(f + k < NF, cnext[k - 1].astype(F32), 0.0).astype(BF16)
        right[1, 0, 0:COLS, k * CH : (k + 1) * CH] = tail
        term = dot_back(right[1, 0, :, k * CH : (k + 1) * CH], tw[k])
        grad = term if grad is None else grad + term
    send(right.at[1, 0], right.at[1, 1], "sib", sibling)

    pl.semaphore_wait(known.at[0], len(ring))
    further = [at_z(2), at_z(NZ - 2), at_y(2), at_y(NY - 2)]
    for device in further:
        greet(device, known.at[1])

    for dr in (-1, 1):
        from_row(vrow, "vrow0", dr)
    for p in range(3):
        dr = p - 1
        rows = (vid[...] if dr == 0 else vrow[0 if dr < 0 else 1]).astype(F32)
        if dr != 0:
            rows = jnp.where(row_ok(dr), rows, 0.0)
        left[0:COLS, p * CH : (p + 1) * CH] = (rows * modv).astype(BF16)

    @pl.when(owner)
    def _():
        for p in range(3):
            dr = p - 1
            pieces = hv.at[pl.ds(0, 9 if dr else 8)]

            @pl.when(row_ok(dr))
            def _():
                wait_arrived("hv0", pieces, p)

            block = head_block(hv[10 * p], joined(hv, 10 * p + 1), hv[10 * p + 9])
            if dr != 0:
                block = jnp.where(row_ok(dr), block, 0.0)
            left[COLS:ROWS, p * CH : (p + 1) * CH] = (block * modv).astype(BF16)

    local(3, wv, wv).wait()

    xs = left[:, 0 : 3 * CH]
    pre = down(dot(xs, wv[0].reshape(3 * CH, CH)))
    pre = pre + dot(xs, wv[1].reshape(3 * CH, CH))
    pre = pre + up(dot(xs, wv[2].reshape(3 * CH, CH)))
    pre = pre + vecs[1]
    sig = jax.nn.sigmoid(pre)
    left[:, 3 * CH : 4 * CH] = (pre * sig).astype(BF16)
    slope = sig * (1.0 + pre * (1.0 - sig))

    half_other = pl.multiple_of(2 * CH * (1 - c), 2 * CH)
    half_mine = pl.multiple_of(2 * CH * c, 2 * CH)
    send(left.at[:, pl.ds(half_other, 2 * CH)], lsib.at[1], "sib", sibling)

    pg16 = (grad.astype(BF16).astype(F32) * slope).astype(BF16)
    pg = pg16.astype(F32)
    right[0, 0, :, CH : 2 * CH] = pg16
    theirs = right.at[0, 1, :, pl.ds(CH, CH)]
    send(right.at[0, 0, :, pl.ds(CH, CH)], theirs, "psib", sibling)
    pgt[...] = pg16[0:COLS]
    pg_own = pg[FIRST : FIRST + OWN]
    pgh[...] = pg_own.astype(BF16)
    pgb[...] = stacked(jnp.where(low, pg_own[OWN - HEAD :], pg_own[:HEAD]))

    def head_rows(ro):
        i = 1 - ro
        return remote(pgh, phr.at[i // 2], SENT["ph0"] + 1 + ro, RECV["ph0"] + i, at(0, ro))

    def head_edge(ro):
        return remote(pgb, phb.at[1 - ro], SENT["ph0"] + 1 + ro, RECV["ph0"] + 1 - ro, (NF - 1 - f, at(0, ro)[1]))

    for ro in (-1, 1):

        @pl.when(row_ok(ro))
        def _():
            to_row(pgt, prow, "prow0", ro).start()

        @pl.when(owner & row_ok(ro))
        def _():
            head_rows(ro).start()

    for ro in (-1, 0, 1):

        @pl.when(owner & row_ok(ro))
        def _():
            head_edge(ro).start()

    right[0, 0, :, 0:CH] = up(pg).astype(BF16)
    right[0, 0, :, 2 * CH : 3 * CH] = down(pg).astype(BF16)
    bias_terms = jnp.sum(pg, axis=0, keepdims=True)
    vec[0] = jnp.concatenate([bias_terms[:, 0:128], bias_terms[:, 128:256], jnp.zeros((2, 128), F32)], axis=0)

    lsib[0] = left[:, pl.ds(half_mine, 2 * CH)]

    def terms(j, core):
        return dot_outer(lsib[core, :, j * CH : (j + 1) * CH], right[0 if j == 0 else c, core])

    for j in range(2):
        prod[j] = terms(j, 0)
    def pair_of_taps(t, lanes=slice(0, CH)):
        parts = [
            prod[tap // 3, :, (tap % 3) * CH + lanes.start : (tap % 3) * CH + lanes.stop].reshape(NX, NZ, 8, -1)
            for tap in (2 * t, 2 * t + 1)
        ]
        return jnp.concatenate(parts, axis=2).astype(BF16)

    def by_x(k, tally=on_both):
        g[k] = pair_of_taps(k // 2, HALVES[k % 2])
        for o in AROUND_X:
            send(g.at[k, lax.rem(x + o, NX)], xb.at[k, o - 1], f"x{k}", at_x(o), tally=tally)

    def last_products():
        prod[1] = prod[1] + terms(1, 1)

    def by_z():
        for i in range(3):
            block = pair_of_taps((3 + i) // 2, HALVES[(3 + i) % 2])
            for j in range(NX):
                gz[:, j, i] = block[j]
        for o in AROUND_8:
            send(gz.at[lax.rem(z + o, NZ)], zfb.at[o - 1], "last1", at_z(o), tally=on_0)

    def by_y():
        for half in range(2):
            gy[half * NX : (half + 1) * NX] = pair_of_taps(2, HALVES[half])
        for o in AROUND_8:
            send(gy.at[lax.rem(y + o, NY)], yfb.at[o - 1], "last1", at_y(o), tally=on_1)

    wait_arrived("sib", sizes.at[pl.ds(0, 140)])
    pl.semaphore_wait(known.at[1], len(further))
    for o in AROUND_X:
        send(vec.at[0], vxb.at[o - 1], "vx", at_x(o), "vec")

    @pl.when(c == 1)
    def _():
        last_products()
        by_y()

    wait_arrived("psib", theirs)
    other = right[0, 1, :, CH : 2 * CH].astype(F32)
    right[0, 1, :, 0:CH] = up(other).astype(BF16)
    right[0, 1, :, 2 * CH : 3 * CH] = down(other).astype(BF16)

    prod[0] = prod[0] + terms(0, 1)
    by_x(0)
    by_x(1)

    @pl.when(c == 0)
    def _():
        last_products()
        by_z()

    by_x(2)

    @pl.when(c == 1)
    def _():
        by_x(3, on_1)

    def weight_rows(tap):
        both = wv[tap % 3, tap // 3, pl.ds(pl.multiple_of(16 * lax.div(r, 2), 16), 16), :].astype(F32)
        return jnp.where(lax.rem(r, 2) == 0, both[:8], both[8:])

    for i in range(6):
        wsel[i] = jnp.where(c == 0, weight_rows(i), weight_rows(6 + i) if i < 3 else 0.0)

    def total_of(own, parts, count):
        acc = own.astype(F32)
        for i in range(count):
            acc = acc + parts[i].astype(F32)
        return acc

    psum[...] = jnp.zeros((8, 128), F32)

    def over_y(k, own, tally=on_both):
        t, lanes = k // 2, HALVES[k % 2]
        psum[...] = psum[...] + (own[0:8] * wsel[2 * t, :, lanes] + own[8:16] * wsel[2 * t + 1, :, lanes])
        yb[y, k] = own.astype(BF16)
        for o in AROUND_8:
            send(yb.at[y, k], yb.at[y, k], "y", at_y(o), tally=tally)

    def vec_left(whole):
        remote(whole, whole, SENT["vec"], 0, sibling).wait_send()

    wait_arrived("vx", vxb)
    vec_left(vxb)
    vec[1] = total_of(vec[0], vxb, NX - 1)
    for o in AROUND_8:
        send(vec.at[1], vzb.at[o - 1], "vz", at_z(o), "vec")

    def x_to_z(k, tally=on_both):
        wait_arrived(f"x{k}", xb.at[k])
        h[k] = total_of(g[k, x], xb.at[k], NX - 1).astype(BF16)
        for o in AROUND_8:
            send(h.at[k, lax.rem(z + o, NZ)], zb.at[k, o - 1], f"z{k}", at_z(o), tally=tally)

    for k in range(3):
        x_to_z(k)

    belongs = lax.rem(y, NX)

    def to_its_row(i):
        return remote(hy.at[i], rows_in.at[r], SENT["odd"], RECV["last2"], (f, belongs * NZ + i))

    @pl.when(c == 0)
    def _():
        wait_arrived("last1", zfb)
        hx[...] = total_of(gz[z], zfb, NZ - 1).astype(BF16)
        for o in AROUND_X:
            send(hx.at[lax.rem(x + o, NX)], xlb.at[o - 1], "last2", at_x(o), tally=on_0)

    @pl.when(c == 1)
    def _():
        x_to_z(3, on_1)
        wait_arrived("last1", yfb)
        hy[...] = total_of(gy[y], yfb, NY - 1).astype(BF16)
        for i in range(NZ):

            @pl.when((x != belongs) | (z != i))
            def _():
                to_its_row(i).start()

        @pl.when(x == belongs)
        def _():
            rows_in[r] = hy[z]

    for dr in (-1, 1):
        from_row(prow, "prow0", dr)
    for p in range(3):
        dr = 1 - p
        if dr == 0:
            rows = pgt[...]
        else:
            rows = prow[0 if dr < 0 else 1].astype(F32)
            rows = jnp.where(row_ok(dr), rows, 0.0).astype(BF16)
        back[p, 0:COLS, :] = rows

    @pl.when(owner)
    def _():
        for p in range(3):
            dr = 1 - p
            @pl.when(row_ok(dr))
            def _():
                wait_arrived("ph0", sizes.at[pl.ds(0, 9 if dr else 1)], dr + 1)

            own = pg_own if dr == 0 else phr[0 if dr < 0 else 1].astype(F32)
            block = head_block(phb[dr + 1], own, phb[dr + 1])
            if dr != 0:
                block = jnp.where(row_ok(dr), block, 0.0)
            back[p, COLS:ROWS, :] = block.astype(BF16)

    convs = []
    for q in range(3):
        acc = None
        for p in range(3):
            term = dot_back(back[p], wv[q, p])
            acc = term if acc is None else acc + term
        convs.append(acc)
    mod_grad = up(convs[0]) + convs[1] + down(convs[2])
    tail_grad = mod_grad[0:COLS]
    head_grad = mod_grad[FIRST : FIRST + OWN]
    gt_v[...] = (cot[...].astype(F32) + modv * tail_grad).astype(BF16)

    def head_result(o):
        to = jnp.where(low, o, NF - 1 - o)
        return remote(ghs.at[lax.rem(to, NF // 2)], ghr, SENT["ph1"], RECV["gh"], (to, r))

    @pl.when(owner)
    def _():
        result = joined(chg, 0) + modv * head_grad
        for k in range(OWN // HEAD):
            ghs[k] = stacked(result[k * HEAD : (k + 1) * HEAD])
        for o in range(1, NF // 2):
            head_result(o).start()
        ghr[...] = ghs[place]

    local(0, gt_v, gt_o).start()

    def z_to_y(k, tally=on_both):
        wait_arrived(f"z{k}", zb.at[k])
        over_y(k, total_of(h[k, z], zb.at[k], NZ - 1), tally)

    def to_all(o):
        half = lax.div(y, NX)
        return remote(ends.at[half], ends.at[half], SENT["odd"], RECV["ends"], at_y(o))

    z_to_y(0)
    z_to_y(1)
    z_to_y(2)

    @pl.when(c == 1)
    def _():
        z_to_y(3, on_1)

    @pl.when(c == 0)
    def _():
        wait_arrived("last2", xlb)
        acc = total_of(hx[x], xlb, NX - 1)
        for i in range(3):
            over_y(3 + i, acc[i], on_0)

    wait_arrived("vz", vzb)
    vec_left(vzb)
    per_row = psum[...]
    per_row = jnp.sum(per_row, axis=1, keepdims=True)
    lanes = lax.broadcasted_iota(jnp.int32, (8, 128), 1)
    in_lanes = jnp.where(lanes == lax.broadcasted_iota(jnp.int32, (8, 128), 0), per_row, 0.0)
    scale_terms = jnp.sum(in_lanes, axis=0, keepdims=True)
    summed = total_of(vec[1], vzb, NZ - 1)
    vyb[f] = jnp.concatenate([summed[0:2], scale_terms, jnp.zeros((1, 128), F32)], axis=0)
    for o in AROUND_8:
        for core in (c, 1 - c):
            send(vyb.at[f], vyb.at[f], "vy", (lax.rem(y + o, NY) * 2 + core, r), "vec")
    send(vyb.at[f], vyb.at[f], "vy", sibling, "vec")
    @pl.when(c == 1)
    def _():
        @pl.when(x != belongs)
        def _():
            wait_left("odd", NZ)

        @pl.when(x == belongs)
        def _():
            wait_left("odd", NZ - 1)
            wait_arrived("last2", rows_in.at[pl.ds(0, NR - 1)])
            ends[lax.div(y, NX)] = total_of(rows_in[0], rows_in.at[pl.ds(1, NR - 1)], NR - 1)
            for o in AROUND_8:
                to_all(o).start()

    wait_arrived("vy", vyb.at[pl.ds(0, NF - 1)])
    both = total_of(vyb[0], vyb.at[pl.ds(1, NF - 1)], NF - 1) * SCALE
    lower = r < NR // 2
    two = jnp.concatenate(
        [
            jnp.where(lower, both[0:1], both[1:2]),
            jnp.where(lower, modv[:, 0:128], modv[:, 128:256]),
            jnp.zeros((6, 128), F32),
        ],
        axis=0,
    )
    turned = pltpu.roll(two, lax.rem(128 - 8 * lax.rem(r, 16), 128), 1)
    gv_v[...] = jnp.concatenate([both[2:3, 0:8] / turned[1:2, 0:8], turned[0:1, 0:8]], axis=0)
    local(2, gv_v, gv_o).start()

    @pl.when(f != mine_at)
    def _():
        wait_arrived("gh", ghr)

    gh_v[...] = unstacked(ghr[...]).astype(BF16)
    local(1, gh_v, gh_o).start()

    @pl.when(c == 0)
    def _():
        wait_arrived("y", yb.at[pl.ds(0, NY - 1)])

    @pl.when(c == 1)
    def _():
        wait_arrived("y", yb.at[pl.ds(0, NY - 1), pl.ds(0, 4)])

        @pl.when(x == belongs)
        def _():
            wait_arrived("ends", ends.at[0])
            wait_left("odd", 2 * (NY - 1))

        @pl.when(x != belongs)
        def _():
            wait_arrived("ends", ends)

    acc = total_of(yb[0], yb.at[pl.ds(1, NY - 1)], NY - 1)
    for t in range(3):
        both = jnp.concatenate([acc[2 * t], acc[2 * t + 1]], axis=1)
        if t == 2:
            both = jnp.where(c == 0, both, jnp.concatenate([ends[0], ends[1]], axis=1))
        total[2 * t : 2 * t + 2] = (both * SCALE).reshape(2, 8, CH)
    send(total, taps_o.at[pl.ds(6 * c, 6)], "total", sibling)
    local(3, total, taps_o.at[pl.ds(6 * c, 6)]).start()
    wait_arrived("total", total)

    @pl.when(c == 0)
    def _():
        wait_left("all", sum(on_both) + sum(on_0))

    @pl.when(c == 1)
    def _():
        wait_left("all", sum(on_both) + sum(on_1))

    vec_left(vyb.at[pl.ds(0, NF - 1)])
    for ro in (-1, 0, 1):
        @pl.when(row_ok(ro) if ro else f != mine_at)
        def _():
            wait_left("up", 33 if ro else 2, 1 + ro)

        @pl.when(middle & row_ok(ro))
        def _():
            wait_left("ph0", 1, 1 + ro)

        @pl.when(owner & row_ok(ro))
        def _():
            wait_left("ph0", 9 if ro else NF // 2, 1 + ro)

    for i, whole in enumerate((gt_v, gh_v, gv_v, total)):
        local(i, whole, whole).wait()


def write_out(gt, gh, taps, gv, gt_o, gh_o, gc_o, gtw_o, gv_o, sems):
    pairs = ((gt, gt_o), (gh, gh_o), (taps.at[pl.ds(0, 9)], gc_o), (taps.at[pl.ds(9, 3)], gtw_o), (gv, gv_o))
    copies = [pltpu.make_async_copy(src, dst, sems.at[i]) for i, (src, dst) in enumerate(pairs)]
    for copy in copies:
        copy.start()
    for copy in copies:
        copy.wait()


def body(video_tail, video_head, cotangent_tail, cotangent_head, modulation, conv_weight, conv_bias, temporal_weight):
    any_spec = pl.BlockSpec(memory_space=pl.ANY)
    scratch = [
        ((2, COLS, CH), BF16), ((2, HEAD, CH), BF16), ((2, 1, CH), F32),
        ((3, 3, CH, CH), BF16), ((3, CH, CH), BF16),
        ((COLS, CH), BF16), ((HEAD, CH), BF16), ((2, 8), F32),
        ((16, 128), BF16), ((16, 128), BF16), ((2, COLS, CH), BF16), ((2, COLS, CH), BF16),
        ((30, 16, 128), BF16), ((NF // 2, 16, 128), BF16),
        ((ROWS, 4 * CH), BF16), ((2, ROWS, 2 * CH), BF16), ((2, 2, ROWS, 3 * CH), BF16),
        ((3, ROWS, CH), BF16), ((2, COLS, CH), BF16), ((COLS, CH), BF16), ((OWN, CH), BF16),
        ((16, 128), BF16), ((2, OWN, CH), BF16), ((3, 16, 128), BF16), ((NF // 2, 16, 128), BF16),
        ((16, 128), BF16), ((6, 8, CH), F32),
        ((2, CH, 3 * CH), F32), ((4, NX, NZ, 16, 128), BF16), ((4, NX - 1, NZ, 16, 128), BF16),
        ((4, NZ, 16, 128), BF16), ((4, NZ - 1, 16, 128), BF16),
        ((NZ, NX, 3, 16, 128), BF16), ((NZ - 1, NX, 3, 16, 128), BF16), ((NX, 3, 16, 128), BF16),
        ((NX - 1, 3, 16, 128), BF16),
        ((NY, NZ, 16, 128), BF16), ((NY - 1, NZ, 16, 128), BF16), ((NZ, 16, 128), BF16), ((NR, 16, 128), BF16),
        ((2, 16, 128), F32), ((8, 128), F32), ((NY, 6, 16, 128), BF16),
        ((6, 8, CH), F32),
        ((2, 4, 128), F32), ((NZ - 1, 4, 128), F32), ((NX - 1, 4, 128), F32), ((NF, 4, 128), F32),
        ((UNITS, 8, 128), F32),
    ]
    shapes = [((COLS, CH), BF16), ((HEAD, CH), BF16), ((9, 8, CH), F32), ((3, 8, CH), F32), ((2, 8), F32)]
    operands = [
        video_tail.reshape(COLS, CH),
        video_head.reshape(HEAD, CH),
        cotangent_tail.reshape(COLS, CH),
        cotangent_head.reshape(HEAD, CH),
        modulation.reshape(1, CH),
        conv_weight.reshape(3, 3, CH, CH),
        conv_bias.reshape(1, CH),
        temporal_weight,
    ]
    outs = pl.pallas_call(
        kernel,
        out_shape=tuple(pltpu.VMEM(shape, kind) for shape, kind in shapes[:2] + [((12, 8, CH), F32), shapes[4]]),
        in_specs=[any_spec] * 8,
        out_specs=(any_spec,) * 4,
        scratch_shapes=[pltpu.VMEM(shape, kind) for shape, kind in scratch]
        + [
            pltpu.SemaphoreType.DMA((5,)),
            pltpu.SemaphoreType.DMA((len(LEAVE),)),
            pltpu.SemaphoreType.DMA((len(ARRIVE),)),
            pltpu.SemaphoreType.REGULAR((2,)),
        ],
        compiler_params=pltpu.CompilerParams(
            collective_id=0, has_side_effects=True, vmem_limit_bytes=40 << 20
        ),
        name="video_block_backward",
    )(*[pltpu.with_memory_space_constraint(a, pltpu.HBM) for a in operands])
    outs = pl.pallas_call(
        write_out,
        out_shape=tuple(jax.ShapeDtypeStruct(shape, kind) for shape, kind in shapes),
        in_specs=[any_spec] * 4,
        out_specs=(any_spec,) * 5,
        scratch_shapes=[pltpu.SemaphoreType.DMA((5,))],
        compiler_params=pltpu.CompilerParams(vmem_limit_bytes=1 << 20),
        name="write_out",
    )(*outs)
    return (outs[0].reshape(1, 1, COLS, CH), outs[1].reshape(1, HEAD, CH), outs[2], outs[3], outs[4])


def solution(mesh):
    return jax.shard_map(
        body,
        mesh=mesh,
        in_specs=(
            P("frame", "row", None, None),
            P("row", "frame", None),
            P("frame", "row", None, None),
            P("row", "frame", None),
            P(),
            P(),
            P(),
            P(),
        ),
        out_specs=(
            P("frame", "row", None, None),
            P("row", "frame", None),
            P(None, "row", None),
            P(None, "row", None),
            P(None, "row"),
        ),
        check_vma=False,
    )
```

```python
import functools
import math

import jax
import jax.numpy as jnp
from jax import lax
from jax.experimental import pallas as pl
from jax.experimental.pallas import tpu as pltpu
from jax.sharding import PartitionSpec as P

MESH = pl.DeviceIdType.MESH
F32 = jnp.float32
BF16 = jnp.bfloat16
COLS = 128
CH = 256
HEAD = 8
OWN = 64
FIRST = COLS + HEAD
ROWS = 224
NX, NY, NZ, NF, NR = 4, 8, 8, 16, 32
AROUND_X = (2, 1, 3)
AROUND_8 = (4, 3, 5, 2, 6, 1, 7)
HALVES = (slice(0, CH // 2), slice(CH // 2, CH))
SCALE = 1.0 / math.sqrt(17 * 32 * 128)


ARRIVE = (
    "vrow0", "vrow1", "cnext", "hv0", "hv1", "hv2", "chg", "prow0", "prow1", "ph0", "ph1", "ph2", "gh",
    "sib", "psib", "total", "x0", "x1", "x2", "x3", "z0", "z1", "z2", "z3", "last1", "last2", "ends", "late1", "late2", "late3", "y", "vz", "vx", "vy",
)
LEAVE = ("all", "up", "same", "down", "ph0", "ph1", "ph2", "vec", "odd", "late")
OVER_Y = (("late1", "late2", "late3", "late"), ("last1", "last2", "ends", "odd"))
UNITS = 448
RECV = {name: i for i, name in enumerate(ARRIVE)}
SENT = {name: i for i, name in enumerate(LEAVE)}


def stacked(piece):
    half = CH // 2
    return jnp.concatenate([piece[..., :half], piece[..., half:]], axis=-2).astype(BF16)


def unstacked(piece):
    rows = piece.astype(F32)
    return jnp.concatenate([rows[:HEAD], rows[HEAD:]], axis=1)


def dot(a, b):
    return jnp.dot(a, b, preferred_element_type=F32)


def dot_back(a, b):
    return lax.dot_general(a, b, (((1,), (1,)), ((), ())), preferred_element_type=F32)


def dot_outer(a, b):
    return lax.dot_general(a, b, (((0,), (0,)), ((), ())), preferred_element_type=F32)


def edge_cleared(v, row):
    if v.shape[0] != COLS:
        return v
    return jnp.where(lax.broadcasted_iota(jnp.int32, v.shape, 0) == row, 0.0, v)


def down(v):
    return edge_cleared(pltpu.roll(v, 1, 0), 0)


def up(v):
    return edge_cleared(pltpu.roll(v, v.shape[0] - 1, 0), COLS - 1)


def kernel(
    vid_h, vh_h, cot_h, ch_h, mod_h, cw_h, cb_h, tw_h,
    gt_o, gh_o, taps_o, gv_o,
    vc, heads, vecs, wv, tw, gt_v, gh_v, gv_v,
    vhs, chs, vrow, cnext, hv, chg,
    left, lsib, right, back, prow, pgt, pgh, pgb, phr, phb, ghs, ghr, wsel,
    grads, prod, g, xb, h, zb, gz, zfb, hx, xlb, gy, yfb, hy, rows_in, ends, psum, yb, total,
    vec, vzb, vxb, vyb,
    sizes, lsem, ss, rs, known,
):
    f = lax.axis_index("frame")
    r = lax.axis_index("row")
    y, c = lax.div(f, 2), lax.rem(f, 2)
    x, z = lax.div(r, NZ), lax.rem(r, NZ)

    def at(fo, ro):
        return (lax.rem(f + fo + NF, NF), lax.rem(r + ro + NR, NR))

    def at_x(o):
        return (f, lax.rem(x + o, NX) * NZ + z)

    def at_z(o):
        return (f, x * NZ + lax.rem(z + o, NZ))

    def at_y(o):
        return (lax.rem(y + o, NY) * 2 + c, r)

    sibling = (y * 2 + 1 - c, r)
    low, high = f == 0, f == NF - 1
    owner = low | high
    with_head = (y == 0) | (y == NY - 1)
    middle = (f == NF // 2 - 1) | (f == NF // 2)
    mine_at = jnp.where(f < NF // 2, 0, NF - 1)
    place = lax.rem(f, NF // 2)

    def remote(src, dst, leave, arrive, device):
        return pltpu.make_async_remote_copy(
            src_ref=src, dst_ref=dst, send_sem=ss.at[leave], recv_sem=rs.at[arrive],
            device_id=device, device_id_type=MESH,
        )

    on_both, on_0, on_1 = [], [], []
    on_rows = {ROWS: [], COLS: []}

    def by_rows(part):
        for rows, here in ((ROWS, with_head), (COLS, jnp.logical_not(with_head))):
            pl.when(here)(functools.partial(part, rows))


    def send(src, dst, name, device, leave="all", tally=on_both):
        remote(src, dst, SENT[leave], RECV[name], device).start()
        if leave == "all":
            tally.append(math.prod(src.shape) * src.dtype.itemsize // 4096)

    def wait_arrived(name, whole, more=0):
        remote(whole, whole, 0, RECV[name] + more, sibling).wait_recv()

    def wait_left(name, count, more=0):
        whole = sizes.at[pl.ds(0, count)]
        remote(whole, whole, SENT[name] + more, 0, sibling).wait_send()

    barrier = pltpu.get_barrier_semaphore()

    def row_ok(ro):
        return (r + ro >= 0) & (r + ro < NR)

    def greet(device, semaphore=barrier):
        pl.semaphore_signal(semaphore, inc=1, device_id=device, device_id_type=MESH)

    rows_beside = jnp.where(row_ok(-1), 1, 0) + jnp.where(row_ok(1), 1, 0)
    for ro in (-1, 1):

        @pl.when(row_ok(ro))
        def _():
            greet(at(0, ro))

    greet(sibling)
    greet(at(1, 0))
    greet(at(2, 0))
    ring = [at_x(1), at_x(NX - 1), at_z(1), at_z(NZ - 1), at_y(1), at_y(NY - 1)]
    for device in ring:
        greet(device)
    for ro in (-1, 0, 1):

        @pl.when(owner & row_ok(ro))
        def _():
            for o in range(0 if ro else 1, NF // 2 + 1):
                greet((jnp.where(low, o, NF - 1 - o), at(0, ro)[1]))
            greet((NF - 1 - f, at(0, ro)[1]))

    greeted = 9 + 2 * rows_beside + jnp.where(f != mine_at, 1, 0) + jnp.where(middle | owner, rows_beside + 1, 0)

    def local(group, src, dst):
        return pltpu.make_async_copy(src, dst, lsem.at[group])

    for group, src, dst in (
        (0, vid_h, vc.at[0]), (0, cot_h, vc.at[1]), (1, vh_h, heads.at[0]), (1, ch_h, heads.at[1]),
        (2, mod_h, vecs.at[0]), (2, cb_h, vecs.at[1]),
        (3, cw_h.at[:, 0], wv.at[0]), (3, cw_h.at[:, 1], wv.at[1]), (3, cw_h.at[:, 2], wv.at[2]),
        (4, tw_h, tw),
    ):
        local(group, src, dst).start()
    for group, whole in ((1, heads), (2, vecs), (0, vc)):
        local(group, whole, whole).wait()
    vid, cot = vc.at[0], vc.at[1]
    vh32, ch32 = heads[0].astype(F32), heads[1].astype(F32)
    vhs[...] = stacked(vh32)
    chs[...] = stacked(ch32)
    left[COLS:ROWS, 0 : 3 * CH] = jnp.zeros((ROWS - COLS, 3 * CH), BF16)
    right[1, 0, COLS:ROWS, :] = jnp.zeros((ROWS - COLS, 3 * CH), BF16)
    back[:, COLS:ROWS, :] = jnp.zeros((3, ROWS - COLS, CH), BF16)
    pl.semaphore_wait(barrier, greeted)
    for device in ring:
        greet(device, known.at[0])

    def head_piece(to, slot, ro, leave):
        return remote(
            vhs, hv.at[10 * (1 - ro) + slot], SENT[leave] + 1 + ro, RECV["hv0"] + 1 - ro, (to, at(0, ro)[1])
        )

    def own_piece(ro):
        return head_piece(mine_at, place + 1, ro, "up")

    def edge_piece(ro):
        return head_piece(NF - 1 - mine_at, jnp.where(f < NF // 2, 0, 9), ro, "ph0")

    def head_cot():
        return remote(chs, chg.at[place], SENT["same"], RECV["chg"], (mine_at, r))

    def to_row(src, dst, name, ro, leave="up"):
        i = (1 - ro) // 2
        return remote(src, dst.at[i], SENT[leave] + 1 + ro, RECV[name] + i, at(0, ro))

    def from_row(dst, name, dr):
        i = (1 + dr) // 2

        @pl.when(row_ok(dr))
        def _():
            wait_arrived(name, dst.at[i], i)

    for ro in (-1, 0, 1):

        @pl.when(row_ok(ro) if ro else f != mine_at)
        def _():
            own_piece(ro).start()

        @pl.when(middle & row_ok(ro))
        def _():
            edge_piece(ro).start()

    @pl.when(f != mine_at)
    def _():
        head_cot().start()

    @pl.when(owner)
    def _():
        hv[10 + place + 1] = vhs[...]
        chg[place] = chs[...]

    for ro in (-1, 1):

        @pl.when(row_ok(ro))
        def _():
            to_row(vid, vrow, "vrow0", ro).start()

    send(cot, cnext.at[0], "cnext", at(-1, 0))
    send(cot, cnext.at[1], "cnext", at(-2, 0))

    row_ids = lax.broadcasted_iota(jnp.int32, (HEAD, CH), 0)
    zero8 = jnp.zeros((HEAD, CH), F32)
    zero16 = jnp.zeros((2 * HEAD, CH), F32)
    modv = vecs[0]

    def joined(buffer, first):
        return jnp.concatenate([unstacked(buffer[first + k]) for k in range(OWN // HEAD)], axis=0)

    def head_block(before, own, after):
        before = jnp.where((row_ids == HEAD - 1) & high, unstacked(before), 0.0)
        after = jnp.where((row_ids == 0) & low, unstacked(after), 0.0)
        return jnp.concatenate([before, own, after, zero16], axis=0)

    local(4, tw, tw).wait()
    wait_arrived("cnext", cnext)

    @pl.when(owner)
    def _():
        wait_arrived("chg", chg.at[pl.ds(0, NF // 2 - 1)])
        heads_of = (
            joined(chg, 0),
            jnp.where(low, cot[0:OWN].astype(F32), cnext[0, OWN:COLS].astype(F32)),
            jnp.where(low, cnext[0, 0:OWN].astype(F32), cnext[1, OWN:COLS].astype(F32)),
        )
        for k in range(3):
            block = jnp.concatenate([zero8, heads_of[k], zero8, zero16], axis=0)
            right[1, 0, COLS:ROWS, k * CH : (k + 1) * CH] = block.astype(BF16)

    for k in range(3):
        tail = cot[...]
        if k > 0:
            tail = jnp.where(f + k < NF, cnext[k - 1].astype(F32), 0.0).astype(BF16)
        right[1, 0, 0:COLS, k * CH : (k + 1) * CH] = tail

    def act_grad(n):
        acc = None
        for k in range(3):
            term = dot_back(right[1, 0, 0:n, k * CH : (k + 1) * CH], tw[k])
            acc = term if acc is None else acc + term
        grads[0:n] = acc
        send(right.at[1, 0, pl.ds(0, n)], right.at[1, 1, pl.ds(0, n)], "sib", sibling, tally=on_rows[n])

    by_rows(act_grad)

    pl.semaphore_wait(known.at[0], len(ring))
    further = [at_z(2), at_z(NZ - 2), at_y(2), at_y(NY - 2)]
    for device in further:
        greet(device, known.at[1])

    for dr in (-1, 1):
        from_row(vrow, "vrow0", dr)
    for p in range(3):
        dr = p - 1
        rows = (vid[...] if dr == 0 else vrow[0 if dr < 0 else 1]).astype(F32)
        if dr != 0:
            rows = jnp.where(row_ok(dr), rows, 0.0)
        left[0:COLS, p * CH : (p + 1) * CH] = (rows * modv).astype(BF16)

    @pl.when(owner)
    def _():
        for p in range(3):
            dr = p - 1
            pieces = hv.at[pl.ds(0, 9 if dr else 8)]

            @pl.when(row_ok(dr))
            def _():
                wait_arrived("hv0", pieces, p)

            block = head_block(hv[10 * p], joined(hv, 10 * p + 1), hv[10 * p + 9])
            if dr != 0:
                block = jnp.where(row_ok(dr), block, 0.0)
            left[COLS:ROWS, p * CH : (p + 1) * CH] = (block * modv).astype(BF16)

    local(3, wv, wv).wait()

    half_other = pl.multiple_of(2 * CH * (1 - c), 2 * CH)
    half_mine = pl.multiple_of(2 * CH * c, 2 * CH)

    def theirs(n):
        return right.at[0, 1, pl.ds(0, n), pl.ds(CH, CH)]

    def terms(j, core, n):
        return dot_outer(lsib[core, 0:n, j * CH : (j + 1) * CH], right[0 if j == 0 else c, core, 0:n])

    def forward(n):
        xs = left[0:n, 0 : 3 * CH]
        pre = down(dot(xs, wv[0].reshape(3 * CH, CH)))
        pre = pre + dot(xs, wv[1].reshape(3 * CH, CH))
        pre = pre + up(dot(xs, wv[2].reshape(3 * CH, CH)))
        pre = pre + vecs[1]
        sig = jax.nn.sigmoid(pre)
        left[0:n, 3 * CH : 4 * CH] = (pre * sig).astype(BF16)
        slope = sig * (1.0 + pre * (1.0 - sig))
        send(
            left.at[pl.ds(0, n), pl.ds(half_other, 2 * CH)], lsib.at[1, pl.ds(0, n)], "sib", sibling, tally=on_rows[n]
        )
        pg16 = (grads[0:n].astype(BF16).astype(F32) * slope).astype(BF16)
        pg = pg16.astype(F32)
        right[0, 0, 0:n, CH : 2 * CH] = pg16
        send(right.at[0, 0, pl.ds(0, n), pl.ds(CH, CH)], theirs(n), "psib", sibling, tally=on_rows[n])
        pgt[...] = pg16[0:COLS]
        if n == ROWS:
            pg_own = pg[FIRST : FIRST + OWN]
            pgh[...] = pg_own.astype(BF16)
            pgb[...] = stacked(jnp.where(low, pg_own[OWN - HEAD :], pg_own[:HEAD]))
        right[0, 0, 0:n, 0:CH] = up(pg).astype(BF16)
        right[0, 0, 0:n, 2 * CH : 3 * CH] = down(pg).astype(BF16)
        bias_terms = jnp.sum(pg, axis=0, keepdims=True)
        vec[0] = jnp.concatenate([bias_terms[:, 0:128], bias_terms[:, 128:256], jnp.zeros((2, 128), F32)], axis=0)
        lsib[0, 0:n] = left[0:n, pl.ds(half_mine, 2 * CH)]

    by_rows(forward)

    def head_rows(ro):
        i = 1 - ro
        return remote(pgh, phr.at[i // 2], SENT["ph0"] + 1 + ro, RECV["ph0"] + i, at(0, ro))

    def head_edge(ro):
        return remote(pgb, phb.at[1 - ro], SENT["ph0"] + 1 + ro, RECV["ph0"] + 1 - ro, (NF - 1 - f, at(0, ro)[1]))

    def own_terms(n):
        for j in range(2):
            prod[j] = terms(j, 0, n)

    by_rows(own_terms)

    def pair_of_taps(t, lanes=slice(0, CH)):
        parts = [
            prod[tap // 3, :, (tap % 3) * CH + lanes.start : (tap % 3) * CH + lanes.stop].reshape(NX, NZ, 8, -1)
            for tap in (2 * t, 2 * t + 1)
        ]
        return jnp.concatenate(parts, axis=2).astype(BF16)

    def by_x(k, tally=on_both):
        g[k] = pair_of_taps(k // 2, HALVES[k % 2])
        for o in AROUND_X:
            send(g.at[k, lax.rem(x + o, NX)], xb.at[k, o - 1], f"x{k}", at_x(o), tally=tally)

    def last_products():
        def add(n):
            prod[1] = prod[1] + terms(1, 1, n)

        by_rows(add)

    def by_z():
        for i in range(2):
            block = pair_of_taps(2, HALVES[i])
            for j in range(NX):
                gz[:, j, i] = block[j]
        for o in AROUND_8:
            send(gz.at[lax.rem(z + o, NZ)], zfb.at[o - 1], "last1", at_z(o), tally=on_0)

    def by_y(i):
        for half in range(2):
            gy[i, half * NX : (half + 1) * NX] = pair_of_taps(1 + i, HALVES[half])
        for o in AROUND_8:
            send(gy.at[i, lax.rem(y + o, NY)], yfb.at[i, o - 1], OVER_Y[i][0], at_y(o), tally=on_1)

    by_rows(lambda n: wait_arrived("sib", sizes.at[pl.ds(0, n * 5 // 8)]))
    pl.semaphore_wait(known.at[1], len(further))
    for o in AROUND_X:
        send(vec.at[0], vxb.at[o - 1], "vx", at_x(o), "vec")

    @pl.when(c == 1)
    def _():
        last_products()
        by_y(1)

    def add_first(n):
        wait_arrived("psib", theirs(n))
        other = right[0, 1, 0:n, CH : 2 * CH].astype(F32)
        right[0, 1, 0:n, 0:CH] = up(other).astype(BF16)
        right[0, 1, 0:n, 2 * CH : 3 * CH] = down(other).astype(BF16)
        prod[0] = prod[0] + terms(0, 1, n)

    by_rows(add_first)

    @pl.when(c == 0)
    def _():
        last_products()
        by_z()

    by_x(0)
    by_x(1)

    @pl.when(c == 0)
    def _():
        by_x(2, on_0)
        by_x(3, on_0)

    @pl.when(c == 1)
    def _():
        by_y(0)


    for ro in (-1, 1):

        @pl.when(row_ok(ro))
        def _():
            to_row(pgt, prow, "prow0", ro).start()

        @pl.when(owner & row_ok(ro))
        def _():
            head_rows(ro).start()

    for ro in (-1, 0, 1):

        @pl.when(owner & row_ok(ro))
        def _():
            head_edge(ro).start()

    def weight_rows(tap):
        both = wv[tap % 3, tap // 3, pl.ds(pl.multiple_of(16 * lax.div(r, 2), 16), 16), :].astype(F32)
        return jnp.where(lax.rem(r, 2) == 0, both[:8], both[8:])

    for i in range(6):
        wsel[i] = jnp.where(c == 0, weight_rows(i), weight_rows(6 + i) if i < 3 else 0.0)

    def total_of(own, parts, count):
        acc = own.astype(F32)
        for i in range(count):
            acc = acc + parts[i].astype(F32)
        return acc

    psum[...] = jnp.zeros((8, 128), F32)

    def over_y(k, own, tally=on_both):
        t, lanes = k // 2, HALVES[k % 2]
        psum[...] = psum[...] + (own[0:8] * wsel[2 * t, :, lanes] + own[8:16] * wsel[2 * t + 1, :, lanes])
        yb[y, k] = own.astype(BF16)
        for o in AROUND_8:
            send(yb.at[y, k], yb.at[y, k], "y", at_y(o), tally=tally)

    def vec_left(whole):
        remote(whole, whole, SENT["vec"], 0, sibling).wait_send()

    wait_arrived("vx", vxb)
    vec_left(vxb)
    vec[1] = total_of(vec[0], vxb, NX - 1)
    for o in AROUND_8:
        send(vec.at[1], vzb.at[o - 1], "vz", at_z(o), "vec")

    def x_to_z(k, tally=on_both):
        wait_arrived(f"x{k}", xb.at[k])
        h[k] = total_of(g[k, x], xb.at[k], NX - 1).astype(BF16)
        for o in AROUND_8:
            send(h.at[k, lax.rem(z + o, NZ)], zb.at[k, o - 1], f"z{k}", at_z(o), tally=tally)

    for k in range(2):
        x_to_z(k)

    belongs = lax.rem(y, NX)
    half_at = lax.div(y, NX)

    def to_its_row(i, to_z):
        _, arrive, _, leave = OVER_Y[i]
        return remote(hy.at[i, to_z], rows_in.at[i, r], SENT[leave], RECV[arrive], (f, belongs * NZ + to_z))

    @pl.when(c == 0)
    def _():
        wait_arrived("last1", zfb)
        hx[...] = total_of(gz[z], zfb, NZ - 1).astype(BF16)
        for o in AROUND_X:
            send(hx.at[lax.rem(x + o, NX)], xlb.at[o - 1], "last2", at_x(o), tally=on_0)
        x_to_z(2, on_0)
        x_to_z(3, on_0)

    @pl.when(c == 1)
    def _():
        for i in (1, 0):
            wait_arrived(OVER_Y[i][0], yfb.at[i])
            hy[i] = total_of(gy[i, y], yfb.at[i], NY - 1).astype(BF16)
            for to_z in range(NZ):

                @pl.when((x != belongs) | (z != to_z))
                def _():
                    to_its_row(i, to_z).start()

            @pl.when(x == belongs)
            def _():
                rows_in[i, r] = hy[i, z]

    def z_to_y(k, tally=on_both):
        wait_arrived(f"z{k}", zb.at[k])
        over_y(k, total_of(h[k, z], zb.at[k], NZ - 1), tally)

    def to_all(i, o):
        _, _, arrive, leave = OVER_Y[i]
        return remote(ends.at[i, half_at], ends.at[i, half_at], SENT[leave], RECV[arrive], at_y(o))

    z_to_y(0)
    z_to_y(1)
    for dr in (-1, 1):
        from_row(prow, "prow0", dr)
    for p in range(3):
        dr = 1 - p
        if dr == 0:
            rows = pgt[...]
        else:
            rows = prow[0 if dr < 0 else 1].astype(F32)
            rows = jnp.where(row_ok(dr), rows, 0.0).astype(BF16)
        back[p, 0:COLS, :] = rows

    @pl.when(owner)
    def _():
        for p in range(3):
            dr = 1 - p
            @pl.when(row_ok(dr))
            def _():
                wait_arrived("ph0", sizes.at[pl.ds(0, 9 if dr else 1)], dr + 1)

            own = pgh[...].astype(F32) if dr == 0 else phr[0 if dr < 0 else 1].astype(F32)
            block = head_block(phb[dr + 1], own, phb[dr + 1])
            if dr != 0:
                block = jnp.where(row_ok(dr), block, 0.0)
            back[p, COLS:ROWS, :] = block.astype(BF16)

    convs = []
    for q in range(3):
        acc = None
        for p in range(3):
            term = dot_back(back[p], wv[q, p])
            acc = term if acc is None else acc + term
        convs.append(acc)
    mod_grad = up(convs[0]) + convs[1] + down(convs[2])
    tail_grad = mod_grad[0:COLS]
    head_grad = mod_grad[FIRST : FIRST + OWN]
    gt_v[...] = (cot[...].astype(F32) + modv * tail_grad).astype(BF16)

    def head_result(o):
        to = jnp.where(low, o, NF - 1 - o)
        return remote(ghs.at[lax.rem(to, NF // 2)], ghr, SENT["ph1"], RECV["gh"], (to, r))

    @pl.when(owner)
    def _():
        result = joined(chg, 0) + modv * head_grad
        for k in range(OWN // HEAD):
            ghs[k] = stacked(result[k * HEAD : (k + 1) * HEAD])
        for o in range(1, NF // 2):
            head_result(o).start()
        ghr[...] = ghs[place]

    local(0, gt_v, gt_o).start()

    @pl.when(c == 0)
    def _():
        z_to_y(2, on_0)
        z_to_y(3, on_0)
        wait_arrived("last2", xlb)
        acc = total_of(hx[x], xlb, NX - 1)
        for i in range(2):
            over_y(4 + i, acc[i], on_0)

    @pl.when(c == 1)
    def _():
        for i in (1, 0):
            _, arrive, _, leave = OVER_Y[i]

            @pl.when(x != belongs)
            def _():
                wait_left(leave, NZ)

            @pl.when(x == belongs)
            def _():
                wait_left(leave, NZ - 1)
                wait_arrived(arrive, rows_in.at[i, pl.ds(0, NR - 1)])
                acc = total_of(rows_in[i, 0], rows_in.at[i, pl.ds(1, NR - 1)], NR - 1)
                ends[i, half_at] = acc
                for o in AROUND_8:
                    to_all(i, o).start()
                lanes = pl.ds(pl.multiple_of(128 * half_at, 128), 128)
                t = 2 * (1 + i)
                psum[...] = psum[...] + (acc[0:8] * wsel[t, :, lanes] + acc[8:16] * wsel[t + 1, :, lanes])

    wait_arrived("vz", vzb)
    vec_left(vzb)
    per_row = psum[...]
    per_row = jnp.sum(per_row, axis=1, keepdims=True)
    lanes = lax.broadcasted_iota(jnp.int32, (8, 128), 1)
    in_lanes = jnp.where(lanes == lax.broadcasted_iota(jnp.int32, (8, 128), 0), per_row, 0.0)
    scale_terms = jnp.sum(in_lanes, axis=0, keepdims=True)
    summed = total_of(vec[1], vzb, NZ - 1)
    vyb[f] = jnp.concatenate([summed[0:2], scale_terms, jnp.zeros((1, 128), F32)], axis=0)
    for o in AROUND_8:
        for core in (c, 1 - c):
            send(vyb.at[f], vyb.at[f], "vy", (lax.rem(y + o, NY) * 2 + core, r), "vec")
    send(vyb.at[f], vyb.at[f], "vy", sibling, "vec")
    wait_arrived("vy", vyb.at[pl.ds(0, NF - 1)])
    both = total_of(vyb[0], vyb.at[pl.ds(1, NF - 1)], NF - 1) * SCALE
    lower = r < NR // 2
    two = jnp.concatenate(
        [
            jnp.where(lower, both[0:1], both[1:2]),
            jnp.where(lower, modv[:, 0:128], modv[:, 128:256]),
            jnp.zeros((6, 128), F32),
        ],
        axis=0,
    )
    turned = pltpu.roll(two, lax.rem(128 - 8 * lax.rem(r, 16), 128), 1)
    gv_v[...] = jnp.concatenate([both[2:3, 0:8] / turned[1:2, 0:8], turned[0:1, 0:8]], axis=0)
    local(2, gv_v, gv_o).start()

    @pl.when(f != mine_at)
    def _():
        wait_arrived("gh", ghr)

    gh_v[...] = unstacked(ghr[...]).astype(BF16)
    local(1, gh_v, gh_o).start()

    @pl.when(c == 0)
    def _():
        wait_arrived("y", yb.at[pl.ds(0, NY - 1)])

    @pl.when(c == 1)
    def _():
        wait_arrived("y", yb.at[pl.ds(0, NY - 1), pl.ds(0, 2)])
        for i in range(2):
            _, _, arrive, leave = OVER_Y[i]

            @pl.when(x == belongs)
            def _():
                wait_arrived(arrive, ends.at[i, 0])
                wait_left(leave, 2 * (NY - 1))

            @pl.when(x != belongs)
            def _():
                wait_arrived(arrive, ends.at[i])

    acc = total_of(yb[0], yb.at[pl.ds(1, NY - 1)], NY - 1)
    for t in range(3):
        both = jnp.concatenate([acc[2 * t], acc[2 * t + 1]], axis=1)
        if t > 0:
            both = jnp.where(c == 0, both, jnp.concatenate([ends[t - 1, 0], ends[t - 1, 1]], axis=1))
        total[2 * t : 2 * t + 2] = (both * SCALE).reshape(2, 8, CH)
    send(total, taps_o.at[pl.ds(6 * c, 6)], "total", sibling)
    local(3, total, taps_o.at[pl.ds(6 * c, 6)]).start()
    wait_arrived("total", total)

    def all_left(n):
        for core, more in ((0, on_0), (1, on_1)):
            pl.when(c == core)(functools.partial(wait_left, "all", sum(on_both) + sum(more) + sum(on_rows[n])))

    by_rows(all_left)
    vec_left(vyb.at[pl.ds(0, NF - 1)])
    for ro in (-1, 0, 1):
        @pl.when(row_ok(ro) if ro else f != mine_at)
        def _():
            wait_left("up", 33 if ro else 2, 1 + ro)

        @pl.when(middle & row_ok(ro))
        def _():
            wait_left("ph0", 1, 1 + ro)

        @pl.when(owner & row_ok(ro))
        def _():
            wait_left("ph0", 9 if ro else NF // 2, 1 + ro)

    for i, whole in enumerate((gt_v, gh_v, gv_v, total)):
        local(i, whole, whole).wait()


def write_out(gt, gh, taps, gv, gt_o, gh_o, gc_o, gtw_o, gv_o, sems):
    pairs = ((gt, gt_o), (gh, gh_o), (taps.at[pl.ds(0, 9)], gc_o), (taps.at[pl.ds(9, 3)], gtw_o), (gv, gv_o))
    copies = [pltpu.make_async_copy(src, dst, sems.at[i]) for i, (src, dst) in enumerate(pairs)]
    for copy in copies:
        copy.start()
    for copy in copies:
        copy.wait()


def body(video_tail, video_head, cotangent_tail, cotangent_head, modulation, conv_weight, conv_bias, temporal_weight):
    any_spec = pl.BlockSpec(memory_space=pl.ANY)
    scratch = [
        ((2, COLS, CH), BF16), ((2, HEAD, CH), BF16), ((2, 1, CH), F32),
        ((3, 3, CH, CH), BF16), ((3, CH, CH), BF16),
        ((COLS, CH), BF16), ((HEAD, CH), BF16), ((2, 8), F32),
        ((16, 128), BF16), ((16, 128), BF16), ((2, COLS, CH), BF16), ((2, COLS, CH), BF16),
        ((30, 16, 128), BF16), ((NF // 2, 16, 128), BF16),
        ((ROWS, 4 * CH), BF16), ((2, ROWS, 2 * CH), BF16), ((2, 2, ROWS, 3 * CH), BF16),
        ((3, ROWS, CH), BF16), ((2, COLS, CH), BF16), ((COLS, CH), BF16), ((OWN, CH), BF16),
        ((16, 128), BF16), ((2, OWN, CH), BF16), ((3, 16, 128), BF16), ((NF // 2, 16, 128), BF16),
        ((16, 128), BF16), ((6, 8, CH), F32),
        ((ROWS, CH), F32), ((2, CH, 3 * CH), F32), ((4, NX, NZ, 16, 128), BF16), ((4, NX - 1, NZ, 16, 128), BF16),
        ((4, NZ, 16, 128), BF16), ((4, NZ - 1, 16, 128), BF16),
        ((NZ, NX, 2, 16, 128), BF16), ((NZ - 1, NX, 2, 16, 128), BF16), ((NX, 2, 16, 128), BF16),
        ((NX - 1, 2, 16, 128), BF16),
        ((2, NY, NZ, 16, 128), BF16), ((2, NY - 1, NZ, 16, 128), BF16), ((2, NZ, 16, 128), BF16),
        ((2, NR, 16, 128), BF16), ((2, 2, 16, 128), F32), ((8, 128), F32), ((NY, 6, 16, 128), BF16),
        ((6, 8, CH), F32),
        ((2, 4, 128), F32), ((NZ - 1, 4, 128), F32), ((NX - 1, 4, 128), F32), ((NF, 4, 128), F32),
        ((UNITS, 8, 128), F32),
    ]
    shapes = [((COLS, CH), BF16), ((HEAD, CH), BF16), ((9, 8, CH), F32), ((3, 8, CH), F32), ((2, 8), F32)]
    operands = [
        video_tail.reshape(COLS, CH),
        video_head.reshape(HEAD, CH),
        cotangent_tail.reshape(COLS, CH),
        cotangent_head.reshape(HEAD, CH),
        modulation.reshape(1, CH),
        conv_weight.reshape(3, 3, CH, CH),
        conv_bias.reshape(1, CH),
        temporal_weight,
    ]
    outs = pl.pallas_call(
        kernel,
        out_shape=tuple(pltpu.VMEM(shape, kind) for shape, kind in shapes[:2] + [((12, 8, CH), F32), shapes[4]]),
        in_specs=[any_spec] * 8,
        out_specs=(any_spec,) * 4,
        scratch_shapes=[pltpu.VMEM(shape, kind) for shape, kind in scratch]
        + [
            pltpu.SemaphoreType.DMA((5,)),
            pltpu.SemaphoreType.DMA((len(LEAVE),)),
            pltpu.SemaphoreType.DMA((len(ARRIVE),)),
            pltpu.SemaphoreType.REGULAR((2,)),
        ],
        compiler_params=pltpu.CompilerParams(
            collective_id=0, has_side_effects=True, vmem_limit_bytes=40 << 20
        ),
        name="video_block_backward",
    )(*[pltpu.with_memory_space_constraint(a, pltpu.HBM) for a in operands])
    outs = pl.pallas_call(
        write_out,
        out_shape=tuple(jax.ShapeDtypeStruct(shape, kind) for shape, kind in shapes),
        in_specs=[any_spec] * 4,
        out_specs=(any_spec,) * 5,
        scratch_shapes=[pltpu.SemaphoreType.DMA((5,))],
        compiler_params=pltpu.CompilerParams(vmem_limit_bytes=1 << 20),
        name="write_out",
    )(*outs)
    return (outs[0].reshape(1, 1, COLS, CH), outs[1].reshape(1, HEAD, CH), outs[2], outs[3], outs[4])


def solution(mesh):
    return jax.shard_map(
        body,
        mesh=mesh,
        in_specs=(
            P("frame", "row", None, None),
            P("row", "frame", None),
            P("frame", "row", None, None),
            P("row", "frame", None),
            P(),
            P(),
            P(),
            P(),
        ),
        out_specs=(
            P("frame", "row", None, None),
            P("row", "frame", None),
            P(None, "row", None),
            P(None, "row", None),
            P(None, "row"),
        ),
        check_vma=False,
    )
```

```python
import functools
import math

import jax
import jax.numpy as jnp
from jax import lax
from jax.experimental import pallas as pl
from jax.experimental.pallas import tpu as pltpu
from jax.sharding import PartitionSpec as P

MESH = pl.DeviceIdType.MESH
F32 = jnp.float32
BF16 = jnp.bfloat16
COLS = 128
CH = 256
HEAD = 8
OWN = 64
FIRST = COLS + HEAD
ROWS = 224
NX, NY, NZ, NF, NR = 4, 8, 8, 16, 32
AROUND_X = (2, 1, 3)
AROUND_8 = (4, 3, 5, 2, 6, 1, 7)
HALVES = (slice(0, CH // 2), slice(CH // 2, CH))
SCALE = 1.0 / math.sqrt(17 * 32 * 128)


ARRIVE = (
    "vrow0", "vrow1", "cnext", "hv0", "hv1", "hv2", "chg", "prow0", "prow1", "ph0", "ph1", "ph2", "gh",
    "sib", "psib", "total", "x0", "x1", "x2", "x3", "z0", "z1", "z2", "z3", "last1", "last2", "ends", "late1", "late2", "late3", "y", "vz", "vx", "vy",
)
LEAVE = ("all", "up", "same", "down", "ph0", "ph1", "ph2", "vec", "odd", "late")
OVER_Y = (("late1", "late2", "late3", "late"), ("last1", "last2", "ends", "odd"))
UNITS = 448
RECV = {name: i for i, name in enumerate(ARRIVE)}
SENT = {name: i for i, name in enumerate(LEAVE)}


def stacked(piece):
    half = CH // 2
    return jnp.concatenate([piece[..., :half], piece[..., half:]], axis=-2).astype(BF16)


def unstacked(piece):
    rows = piece.astype(F32)
    return jnp.concatenate([rows[:HEAD], rows[HEAD:]], axis=1)


def dot(a, b):
    return jnp.dot(a, b, preferred_element_type=F32)


def dot_back(a, b):
    return lax.dot_general(a, b, (((1,), (1,)), ((), ())), preferred_element_type=F32)


def dot_outer(a, b):
    return lax.dot_general(a, b, (((0,), (0,)), ((), ())), preferred_element_type=F32)


def edge_cleared(v, row):
    if v.shape[0] != COLS:
        return v
    return jnp.where(lax.broadcasted_iota(jnp.int32, v.shape, 0) == row, 0.0, v)


def down(v):
    return edge_cleared(pltpu.roll(v, 1, 0), 0)


def up(v):
    return edge_cleared(pltpu.roll(v, v.shape[0] - 1, 0), COLS - 1)


def kernel(
    vid_h, vh_h, cot_h, ch_h, mod_h, cw_h, cb_h, tw_h,
    gt_o, gh_o, taps_o, gv_o,
    vc, heads, vecs, wv, tw, gt_v, gh_v, gv_v,
    vhs, chs, vrow, cnext, hv, chg,
    left, lsib, right, back, prow, pgt, pgh, pgb, phr, phb, ghs, ghr, wsel,
    grads, prod, g, xb, h, zb, gz, zfb, hx, xlb, gy, yfb, hy, rows_in, ends, psum, yb, total,
    vec, vzb, vxb, vyb,
    sizes, lsem, ss, rs, known,
):
    f = lax.axis_index("frame")
    r = lax.axis_index("row")
    y, c = lax.div(f, 2), lax.rem(f, 2)
    x, z = lax.div(r, NZ), lax.rem(r, NZ)

    def at(fo, ro):
        return (lax.rem(f + fo + NF, NF), lax.rem(r + ro + NR, NR))

    def at_x(o):
        return (f, lax.rem(x + o, NX) * NZ + z)

    def at_z(o):
        return (f, x * NZ + lax.rem(z + o, NZ))

    def at_y(o):
        return (lax.rem(y + o, NY) * 2 + c, r)

    sibling = (y * 2 + 1 - c, r)
    low, high = f == 0, f == NF - 1
    owner = low | high
    with_head = (y == 0) | (y == NY - 1)
    middle = (f == NF // 2 - 1) | (f == NF // 2)
    mine_at = jnp.where(f < NF // 2, 0, NF - 1)
    place = lax.rem(f, NF // 2)

    def remote(src, dst, leave, arrive, device):
        return pltpu.make_async_remote_copy(
            src_ref=src, dst_ref=dst, send_sem=ss.at[leave], recv_sem=rs.at[arrive],
            device_id=device, device_id_type=MESH,
        )

    on_both, on_0, on_1 = [], [], []
    on_rows = {ROWS: [], COLS: []}

    def by_rows(part):
        for rows, here in ((ROWS, with_head), (COLS, jnp.logical_not(with_head))):
            pl.when(here)(functools.partial(part, rows))


    def send(src, dst, name, device, leave="all", tally=on_both):
        remote(src, dst, SENT[leave], RECV[name], device).start()
        if leave == "all":
            tally.append(math.prod(src.shape) * src.dtype.itemsize // 4096)

    def wait_arrived(name, whole, more=0):
        remote(whole, whole, 0, RECV[name] + more, sibling).wait_recv()

    def wait_left(name, count, more=0):
        whole = sizes.at[pl.ds(0, count)]
        remote(whole, whole, SENT[name] + more, 0, sibling).wait_send()

    barrier = pltpu.get_barrier_semaphore()

    def row_ok(ro):
        return (r + ro >= 0) & (r + ro < NR)

    def greet(device, semaphore=barrier):
        pl.semaphore_signal(semaphore, inc=1, device_id=device, device_id_type=MESH)

    rows_beside = jnp.where(row_ok(-1), 1, 0) + jnp.where(row_ok(1), 1, 0)
    for ro in (-1, 1):

        @pl.when(row_ok(ro))
        def _():
            greet(at(0, ro))

    greet(sibling)
    greet(at(1, 0))
    greet(at(2, 0))
    ring = [at_x(1), at_x(NX - 1), at_z(1), at_z(NZ - 1), at_y(1), at_y(NY - 1)]
    for device in ring:
        greet(device)
    for ro in (-1, 0, 1):

        @pl.when(owner & row_ok(ro))
        def _():
            for o in range(0 if ro else 1, NF // 2 + 1):
                greet((jnp.where(low, o, NF - 1 - o), at(0, ro)[1]))
            greet((NF - 1 - f, at(0, ro)[1]))

    greeted = 9 + 2 * rows_beside + jnp.where(f != mine_at, 1, 0) + jnp.where(middle | owner, rows_beside + 1, 0)

    def local(group, src, dst):
        return pltpu.make_async_copy(src, dst, lsem.at[group])

    for group, src, dst in (
        (0, vid_h, vc.at[0]), (0, cot_h, vc.at[1]), (1, vh_h, heads.at[0]), (1, ch_h, heads.at[1]),
        (2, mod_h, vecs.at[0]), (2, cb_h, vecs.at[1]),
        (3, cw_h.at[:, 0], wv.at[0]), (3, cw_h.at[:, 1], wv.at[1]), (3, cw_h.at[:, 2], wv.at[2]),
        (4, tw_h, tw),
    ):
        local(group, src, dst).start()
    for group, whole in ((1, heads), (2, vecs), (0, vc)):
        local(group, whole, whole).wait()
    vid, cot = vc.at[0], vc.at[1]
    vh32, ch32 = heads[0].astype(F32), heads[1].astype(F32)
    vhs[...] = stacked(vh32)
    chs[...] = stacked(ch32)
    left[COLS:ROWS, 0 : 3 * CH] = jnp.zeros((ROWS - COLS, 3 * CH), BF16)
    right[1, 0, COLS:ROWS, :] = jnp.zeros((ROWS - COLS, 3 * CH), BF16)
    back[:, COLS:ROWS, :] = jnp.zeros((3, ROWS - COLS, CH), BF16)
    pl.semaphore_wait(barrier, greeted)
    for device in ring:
        greet(device, known.at[0])

    def head_piece(to, slot, ro, leave):
        return remote(
            vhs, hv.at[10 * (1 - ro) + slot], SENT[leave] + 1 + ro, RECV["hv0"] + 1 - ro, (to, at(0, ro)[1])
        )

    def own_piece(ro):
        return head_piece(mine_at, place + 1, ro, "up")

    def edge_piece(ro):
        return head_piece(NF - 1 - mine_at, jnp.where(f < NF // 2, 0, 9), ro, "ph0")

    def head_cot():
        return remote(chs, chg.at[place], SENT["same"], RECV["chg"], (mine_at, r))

    def to_row(src, dst, name, ro, leave="up"):
        i = (1 - ro) // 2
        return remote(src, dst.at[i], SENT[leave] + 1 + ro, RECV[name] + i, at(0, ro))

    def from_row(dst, name, dr):
        i = (1 + dr) // 2

        @pl.when(row_ok(dr))
        def _():
            wait_arrived(name, dst.at[i], i)

    for ro in (-1, 0, 1):

        @pl.when(row_ok(ro) if ro else f != mine_at)
        def _():
            own_piece(ro).start()

        @pl.when(middle & row_ok(ro))
        def _():
            edge_piece(ro).start()

    @pl.when(f != mine_at)
    def _():
        head_cot().start()

    @pl.when(owner)
    def _():
        hv[10 + place + 1] = vhs[...]
        chg[place] = chs[...]

    for ro in (-1, 1):

        @pl.when(row_ok(ro))
        def _():
            to_row(vid, vrow, "vrow0", ro).start()

    send(cot, cnext.at[0], "cnext", at(-1, 0))
    send(cot, cnext.at[1], "cnext", at(-2, 0))

    row_ids = lax.broadcasted_iota(jnp.int32, (HEAD, CH), 0)
    zero8 = jnp.zeros((HEAD, CH), F32)
    zero16 = jnp.zeros((2 * HEAD, CH), F32)
    modv = vecs[0]

    def joined(buffer, first):
        return jnp.concatenate([unstacked(buffer[first + k]) for k in range(OWN // HEAD)], axis=0)

    def head_block(before, own, after):
        before = jnp.where((row_ids == HEAD - 1) & high, unstacked(before), 0.0)
        after = jnp.where((row_ids == 0) & low, unstacked(after), 0.0)
        return jnp.concatenate([before, own, after, zero16], axis=0)

    local(4, tw, tw).wait()
    wait_arrived("cnext", cnext)

    @pl.when(owner)
    def _():
        wait_arrived("chg", chg.at[pl.ds(0, NF // 2 - 1)])
        heads_of = (
            joined(chg, 0),
            jnp.where(low, cot[0:OWN].astype(F32), cnext[0, OWN:COLS].astype(F32)),
            jnp.where(low, cnext[0, 0:OWN].astype(F32), cnext[1, OWN:COLS].astype(F32)),
        )
        for k in range(3):
            block = jnp.concatenate([zero8, heads_of[k], zero8, zero16], axis=0)
            right[1, 0, COLS:ROWS, k * CH : (k + 1) * CH] = block.astype(BF16)

    for k in range(3):
        tail = cot[...]
        if k > 0:
            tail = jnp.where(f + k < NF, cnext[k - 1].astype(F32), 0.0).astype(BF16)
        right[1, 0, 0:COLS, k * CH : (k + 1) * CH] = tail

    def act_grad(n):
        acc = None
        for k in range(3):
            term = dot_back(right[1, 0, 0:n, k * CH : (k + 1) * CH], tw[k])
            acc = term if acc is None else acc + term
        grads[0:n] = acc
        send(right.at[1, 0, pl.ds(0, n)], right.at[1, 1, pl.ds(0, n)], "sib", sibling, tally=on_rows[n])

    by_rows(act_grad)

    pl.semaphore_wait(known.at[0], len(ring))
    further = [at_z(2), at_z(NZ - 2), at_y(2), at_y(NY - 2)]
    for device in further:
        greet(device, known.at[1])

    for dr in (-1, 1):
        from_row(vrow, "vrow0", dr)
    for p in range(3):
        dr = p - 1
        rows = (vid[...] if dr == 0 else vrow[0 if dr < 0 else 1]).astype(F32)
        if dr != 0:
            rows = jnp.where(row_ok(dr), rows, 0.0)
        left[0:COLS, p * CH : (p + 1) * CH] = (rows * modv).astype(BF16)

    @pl.when(owner)
    def _():
        for p in range(3):
            dr = p - 1
            pieces = hv.at[pl.ds(0, 9 if dr else 8)]

            @pl.when(row_ok(dr))
            def _():
                wait_arrived("hv0", pieces, p)

            block = head_block(hv[10 * p], joined(hv, 10 * p + 1), hv[10 * p + 9])
            if dr != 0:
                block = jnp.where(row_ok(dr), block, 0.0)
            left[COLS:ROWS, p * CH : (p + 1) * CH] = (block * modv).astype(BF16)

    local(3, wv, wv).wait()

    half_other = pl.multiple_of(2 * CH * (1 - c), 2 * CH)
    half_mine = pl.multiple_of(2 * CH * c, 2 * CH)

    def theirs(n):
        return right.at[0, 1, pl.ds(0, n), pl.ds(CH, CH)]

    def terms(j, core, n):
        return dot_outer(lsib[core, 0:n, j * CH : (j + 1) * CH], right[0 if j == 0 else c, core, 0:n])

    def forward(n):
        xs = left[0:n, 0 : 3 * CH]
        pre = down(dot(xs, wv[0].reshape(3 * CH, CH)))
        pre = pre + dot(xs, wv[1].reshape(3 * CH, CH))
        pre = pre + up(dot(xs, wv[2].reshape(3 * CH, CH)))
        pre = pre + vecs[1]
        sig = jax.nn.sigmoid(pre)
        left[0:n, 3 * CH : 4 * CH] = (pre * sig).astype(BF16)
        slope = sig * (1.0 + pre * (1.0 - sig))
        send(
            left.at[pl.ds(0, n), pl.ds(half_other, 2 * CH)], lsib.at[1, pl.ds(0, n)], "sib", sibling, tally=on_rows[n]
        )
        pg16 = (grads[0:n].astype(BF16).astype(F32) * slope).astype(BF16)
        pg = pg16.astype(F32)
        right[0, 0, 0:n, CH : 2 * CH] = pg16
        send(right.at[0, 0, pl.ds(0, n), pl.ds(CH, CH)], theirs(n), "psib", sibling, tally=on_rows[n])
        pgt[...] = pg16[0:COLS]
        if n == ROWS:
            pg_own = pg[FIRST : FIRST + OWN]
            pgh[...] = pg_own.astype(BF16)
            pgb[...] = stacked(jnp.where(low, pg_own[OWN - HEAD :], pg_own[:HEAD]))
        right[0, 0, 0:n, 0:CH] = up(pg).astype(BF16)
        right[0, 0, 0:n, 2 * CH : 3 * CH] = down(pg).astype(BF16)
        bias_terms = jnp.sum(pg, axis=0, keepdims=True)
        vec[0] = jnp.concatenate([bias_terms[:, 0:128], bias_terms[:, 128:256], jnp.zeros((2, 128), F32)], axis=0)
        lsib[0, 0:n] = left[0:n, pl.ds(half_mine, 2 * CH)]

    by_rows(forward)

    def head_rows(ro):
        i = 1 - ro
        return remote(pgh, phr.at[i // 2], SENT["ph0"] + 1 + ro, RECV["ph0"] + i, at(0, ro))

    def head_edge(ro):
        return remote(pgb, phb.at[1 - ro], SENT["ph0"] + 1 + ro, RECV["ph0"] + 1 - ro, (NF - 1 - f, at(0, ro)[1]))

    def own_terms(n):
        for j in range(2):
            prod[j] = terms(j, 0, n)

    by_rows(own_terms)

    def pair_of_taps(t, lanes=slice(0, CH)):
        parts = [
            prod[tap // 3, :, (tap % 3) * CH + lanes.start : (tap % 3) * CH + lanes.stop].reshape(NX, NZ, 8, -1)
            for tap in (2 * t, 2 * t + 1)
        ]
        return jnp.concatenate(parts, axis=2).astype(BF16)

    def by_x(k, tally=on_both):
        g[k] = pair_of_taps(k // 2, HALVES[k % 2])
        for o in AROUND_X:
            send(g.at[k, lax.rem(x + o, NX)], xb.at[k, o - 1], f"x{k}", at_x(o), tally=tally)

    def last_products():
        def add(n):
            prod[1] = prod[1] + terms(1, 1, n)

        by_rows(add)

    def by_z():
        for i in range(2):
            block = pair_of_taps(2, HALVES[i])
            for j in range(NX):
                gz[:, j, i] = block[j]
        for o in AROUND_8:
            send(gz.at[lax.rem(z + o, NZ)], zfb.at[o - 1], "last1", at_z(o), tally=on_0)

    def by_y(i):
        for half in range(2):
            gy[i, half * NX : (half + 1) * NX] = pair_of_taps(1 + i, HALVES[half])
        for o in AROUND_8:
            send(gy.at[i, lax.rem(y + o, NY)], yfb.at[i, o - 1], OVER_Y[i][0], at_y(o), tally=on_1)

    by_rows(lambda n: wait_arrived("sib", sizes.at[pl.ds(0, n * 5 // 8)]))
    pl.semaphore_wait(known.at[1], len(further))
    for o in AROUND_X:
        send(vec.at[0], vxb.at[o - 1], "vx", at_x(o), "vec")

    @pl.when(c == 1)
    def _():
        last_products()
        by_y(1)

    def add_first(n):
        wait_arrived("psib", theirs(n))
        other = right[0, 1, 0:n, CH : 2 * CH].astype(F32)
        right[0, 1, 0:n, 0:CH] = up(other).astype(BF16)
        right[0, 1, 0:n, 2 * CH : 3 * CH] = down(other).astype(BF16)
        prod[0] = prod[0] + terms(0, 1, n)

    by_rows(add_first)

    @pl.when(c == 0)
    def _():
        last_products()
        by_z()

    by_x(0)
    by_x(1)

    @pl.when(c == 0)
    def _():
        by_x(2, on_0)
        by_x(3, on_0)

    @pl.when(c == 1)
    def _():
        by_y(0)


    for ro in (-1, 1):

        @pl.when(row_ok(ro))
        def _():
            to_row(pgt, prow, "prow0", ro).start()

        @pl.when(owner & row_ok(ro))
        def _():
            head_rows(ro).start()

    for ro in (-1, 0, 1):

        @pl.when(owner & row_ok(ro))
        def _():
            head_edge(ro).start()

    def weight_rows(tap):
        both = wv[tap % 3, tap // 3, pl.ds(pl.multiple_of(16 * lax.div(r, 2), 16), 16), :].astype(F32)
        return jnp.where(lax.rem(r, 2) == 0, both[:8], both[8:])

    for i in range(6):
        wsel[i] = jnp.where(c == 0, weight_rows(i), weight_rows(6 + i) if i < 3 else 0.0)

    def total_of(own, parts, count):
        acc = own.astype(F32)
        for i in range(count):
            acc = acc + parts[i].astype(F32)
        return acc

    psum[...] = jnp.zeros((8, 128), F32)

    def over_y(k, own, tally=on_both):
        t, lanes = k // 2, HALVES[k % 2]
        psum[...] = psum[...] + (own[0:8] * wsel[2 * t, :, lanes] + own[8:16] * wsel[2 * t + 1, :, lanes])
        yb[y, k] = own.astype(BF16)
        for o in AROUND_8:
            send(yb.at[y, k], yb.at[y, k], "y", at_y(o), tally=tally)

    def vec_left(whole):
        remote(whole, whole, SENT["vec"], 0, sibling).wait_send()

    wait_arrived("vx", vxb)
    vec_left(vxb)
    vec[1] = total_of(vec[0], vxb, NX - 1)
    for o in AROUND_8:
        send(vec.at[1], vzb.at[o - 1], "vz", at_z(o), "vec")

    def x_to_z(k, tally=on_both):
        wait_arrived(f"x{k}", xb.at[k])
        h[k] = total_of(g[k, x], xb.at[k], NX - 1).astype(BF16)
        for o in AROUND_8:
            send(h.at[k, lax.rem(z + o, NZ)], zb.at[k, o - 1], f"z{k}", at_z(o), tally=tally)

    for k in range(2):
        x_to_z(k)

    belongs = lax.rem(y, NX)
    half_at = lax.div(y, NX)

    def to_its_row(i, to_z):
        _, arrive, _, leave = OVER_Y[i]
        return remote(hy.at[i, to_z], rows_in.at[i, r], SENT[leave], RECV[arrive], (f, belongs * NZ + to_z))

    @pl.when(c == 0)
    def _():
        wait_arrived("last1", zfb)
        hx[...] = total_of(gz[z], zfb, NZ - 1).astype(BF16)
        for o in AROUND_X:
            send(hx.at[lax.rem(x + o, NX)], xlb.at[o - 1], "last2", at_x(o), tally=on_0)
        x_to_z(2, on_0)
        x_to_z(3, on_0)

    @pl.when(c == 1)
    def _():
        for i in (1, 0):
            wait_arrived(OVER_Y[i][0], yfb.at[i])
            hy[i] = total_of(gy[i, y], yfb.at[i], NY - 1).astype(BF16)
            for to_z in range(NZ):

                @pl.when((x != belongs) | (z != to_z))
                def _():
                    to_its_row(i, to_z).start()

            @pl.when(x == belongs)
            def _():
                rows_in[i, r] = hy[i, z]

    def z_to_y(k, tally=on_both):
        wait_arrived(f"z{k}", zb.at[k])
        over_y(k, total_of(h[k, z], zb.at[k], NZ - 1), tally)

    def to_all(i, o):
        _, _, arrive, leave = OVER_Y[i]
        return remote(ends.at[i, half_at], ends.at[i, half_at], SENT[leave], RECV[arrive], at_y(o))

    z_to_y(0)
    z_to_y(1)

    @pl.when(c == 0)
    def _():
        z_to_y(2, on_0)
        z_to_y(3, on_0)
        wait_arrived("last2", xlb)
        acc = total_of(hx[x], xlb, NX - 1)
        for i in range(2):
            over_y(4 + i, acc[i], on_0)

    @pl.when(c == 1)
    def _():
        for i in (1, 0):
            _, arrive, _, leave = OVER_Y[i]

            @pl.when(x != belongs)
            def _():
                wait_left(leave, NZ)

            @pl.when(x == belongs)
            def _():
                wait_left(leave, NZ - 1)
                wait_arrived(arrive, rows_in.at[i, pl.ds(0, NR - 1)])
                acc = total_of(rows_in[i, 0], rows_in.at[i, pl.ds(1, NR - 1)], NR - 1)
                ends[i, half_at] = acc
                for o in AROUND_8:
                    to_all(i, o).start()
                lanes = pl.ds(pl.multiple_of(128 * half_at, 128), 128)
                t = 2 * (1 + i)
                psum[...] = psum[...] + (acc[0:8] * wsel[t, :, lanes] + acc[8:16] * wsel[t + 1, :, lanes])

    wait_arrived("vz", vzb)
    vec_left(vzb)
    per_row = psum[...]
    per_row = jnp.sum(per_row, axis=1, keepdims=True)
    lanes = lax.broadcasted_iota(jnp.int32, (8, 128), 1)
    in_lanes = jnp.where(lanes == lax.broadcasted_iota(jnp.int32, (8, 128), 0), per_row, 0.0)
    scale_terms = jnp.sum(in_lanes, axis=0, keepdims=True)
    summed = total_of(vec[1], vzb, NZ - 1)
    vyb[f] = jnp.concatenate([summed[0:2], scale_terms, jnp.zeros((1, 128), F32)], axis=0)
    for o in AROUND_8:
        for core in (c, 1 - c):
            send(vyb.at[f], vyb.at[f], "vy", (lax.rem(y + o, NY) * 2 + core, r), "vec")
    send(vyb.at[f], vyb.at[f], "vy", sibling, "vec")
    for dr in (-1, 1):
        from_row(prow, "prow0", dr)
    for p in range(3):
        dr = 1 - p
        if dr == 0:
            rows = pgt[...]
        else:
            rows = prow[0 if dr < 0 else 1].astype(F32)
            rows = jnp.where(row_ok(dr), rows, 0.0).astype(BF16)
        back[p, 0:COLS, :] = rows

    @pl.when(owner)
    def _():
        for p in range(3):
            dr = 1 - p
            @pl.when(row_ok(dr))
            def _():
                wait_arrived("ph0", sizes.at[pl.ds(0, 9 if dr else 1)], dr + 1)

            own = pgh[...].astype(F32) if dr == 0 else phr[0 if dr < 0 else 1].astype(F32)
            block = head_block(phb[dr + 1], own, phb[dr + 1])
            if dr != 0:
                block = jnp.where(row_ok(dr), block, 0.0)
            back[p, COLS:ROWS, :] = block.astype(BF16)

    convs = []
    for q in range(3):
        acc = None
        for p in range(3):
            term = dot_back(back[p], wv[q, p])
            acc = term if acc is None else acc + term
        convs.append(acc)
    mod_grad = up(convs[0]) + convs[1] + down(convs[2])
    tail_grad = mod_grad[0:COLS]
    head_grad = mod_grad[FIRST : FIRST + OWN]
    gt_v[...] = (cot[...].astype(F32) + modv * tail_grad).astype(BF16)

    def head_result(o):
        to = jnp.where(low, o, NF - 1 - o)
        return remote(ghs.at[lax.rem(to, NF // 2)], ghr, SENT["ph1"], RECV["gh"], (to, r))

    @pl.when(owner)
    def _():
        result = joined(chg, 0) + modv * head_grad
        for k in range(OWN // HEAD):
            ghs[k] = stacked(result[k * HEAD : (k + 1) * HEAD])
        for o in range(1, NF // 2):
            head_result(o).start()
        ghr[...] = ghs[place]

    local(0, gt_v, gt_o).start()

    wait_arrived("vy", vyb.at[pl.ds(0, NF - 1)])
    both = total_of(vyb[0], vyb.at[pl.ds(1, NF - 1)], NF - 1) * SCALE
    lower = r < NR // 2
    two = jnp.concatenate(
        [
            jnp.where(lower, both[0:1], both[1:2]),
            jnp.where(lower, modv[:, 0:128], modv[:, 128:256]),
            jnp.zeros((6, 128), F32),
        ],
        axis=0,
    )
    turned = pltpu.roll(two, lax.rem(128 - 8 * lax.rem(r, 16), 128), 1)
    gv_v[...] = jnp.concatenate([both[2:3, 0:8] / turned[1:2, 0:8], turned[0:1, 0:8]], axis=0)
    local(2, gv_v, gv_o).start()

    @pl.when(f != mine_at)
    def _():
        wait_arrived("gh", ghr)

    gh_v[...] = unstacked(ghr[...]).astype(BF16)
    local(1, gh_v, gh_o).start()

    @pl.when(c == 0)
    def _():
        wait_arrived("y", yb.at[pl.ds(0, NY - 1)])

    @pl.when(c == 1)
    def _():
        wait_arrived("y", yb.at[pl.ds(0, NY - 1), pl.ds(0, 2)])
        for i in range(2):
            _, _, arrive, leave = OVER_Y[i]

            @pl.when(x == belongs)
            def _():
                wait_arrived(arrive, ends.at[i, 0])
                wait_left(leave, 2 * (NY - 1))

            @pl.when(x != belongs)
            def _():
                wait_arrived(arrive, ends.at[i])

    acc = total_of(yb[0], yb.at[pl.ds(1, NY - 1)], NY - 1)
    for t in range(3):
        both = jnp.concatenate([acc[2 * t], acc[2 * t + 1]], axis=1)
        if t > 0:
            both = jnp.where(c == 0, both, jnp.concatenate([ends[t - 1, 0], ends[t - 1, 1]], axis=1))
        total[2 * t : 2 * t + 2] = (both * SCALE).reshape(2, 8, CH)
    send(total, taps_o.at[pl.ds(6 * c, 6)], "total", sibling)
    local(3, total, taps_o.at[pl.ds(6 * c, 6)]).start()
    wait_arrived("total", total)

    def all_left(n):
        for core, more in ((0, on_0), (1, on_1)):
            pl.when(c == core)(functools.partial(wait_left, "all", sum(on_both) + sum(more) + sum(on_rows[n])))

    by_rows(all_left)
    vec_left(vyb.at[pl.ds(0, NF - 1)])
    for ro in (-1, 0, 1):
        @pl.when(row_ok(ro) if ro else f != mine_at)
        def _():
            wait_left("up", 33 if ro else 2, 1 + ro)

        @pl.when(middle & row_ok(ro))
        def _():
            wait_left("ph0", 1, 1 + ro)

        @pl.when(owner & row_ok(ro))
        def _():
            wait_left("ph0", 9 if ro else NF // 2, 1 + ro)

    for i, whole in enumerate((gt_v, gh_v, gv_v, total)):
        local(i, whole, whole).wait()


def write_out(gt, gh, taps, gv, gt_o, gh_o, gc_o, gtw_o, gv_o, sems):
    pairs = ((gt, gt_o), (gh, gh_o), (taps.at[pl.ds(0, 9)], gc_o), (taps.at[pl.ds(9, 3)], gtw_o), (gv, gv_o))
    copies = [pltpu.make_async_copy(src, dst, sems.at[i]) for i, (src, dst) in enumerate(pairs)]
    for copy in copies:
        copy.start()
    for copy in copies:
        copy.wait()


def body(video_tail, video_head, cotangent_tail, cotangent_head, modulation, conv_weight, conv_bias, temporal_weight):
    any_spec = pl.BlockSpec(memory_space=pl.ANY)
    scratch = [
        ((2, COLS, CH), BF16), ((2, HEAD, CH), BF16), ((2, 1, CH), F32),
        ((3, 3, CH, CH), BF16), ((3, CH, CH), BF16),
        ((COLS, CH), BF16), ((HEAD, CH), BF16), ((2, 8), F32),
        ((16, 128), BF16), ((16, 128), BF16), ((2, COLS, CH), BF16), ((2, COLS, CH), BF16),
        ((30, 16, 128), BF16), ((NF // 2, 16, 128), BF16),
        ((ROWS, 4 * CH), BF16), ((2, ROWS, 2 * CH), BF16), ((2, 2, ROWS, 3 * CH), BF16),
        ((3, ROWS, CH), BF16), ((2, COLS, CH), BF16), ((COLS, CH), BF16), ((OWN, CH), BF16),
        ((16, 128), BF16), ((2, OWN, CH), BF16), ((3, 16, 128), BF16), ((NF // 2, 16, 128), BF16),
        ((16, 128), BF16), ((6, 8, CH), F32),
        ((ROWS, CH), F32), ((2, CH, 3 * CH), F32), ((4, NX, NZ, 16, 128), BF16), ((4, NX - 1, NZ, 16, 128), BF16),
        ((4, NZ, 16, 128), BF16), ((4, NZ - 1, 16, 128), BF16),
        ((NZ, NX, 2, 16, 128), BF16), ((NZ - 1, NX, 2, 16, 128), BF16), ((NX, 2, 16, 128), BF16),
        ((NX - 1, 2, 16, 128), BF16),
        ((2, NY, NZ, 16, 128), BF16), ((2, NY - 1, NZ, 16, 128), BF16), ((2, NZ, 16, 128), BF16),
        ((2, NR, 16, 128), BF16), ((2, 2, 16, 128), F32), ((8, 128), F32), ((NY, 6, 16, 128), BF16),
        ((6, 8, CH), F32),
        ((2, 4, 128), F32), ((NZ - 1, 4, 128), F32), ((NX - 1, 4, 128), F32), ((NF, 4, 128), F32),
        ((UNITS, 8, 128), F32),
    ]
    shapes = [((COLS, CH), BF16), ((HEAD, CH), BF16), ((9, 8, CH), F32), ((3, 8, CH), F32), ((2, 8), F32)]
    operands = [
        video_tail.reshape(COLS, CH),
        video_head.reshape(HEAD, CH),
        cotangent_tail.reshape(COLS, CH),
        cotangent_head.reshape(HEAD, CH),
        modulation.reshape(1, CH),
        conv_weight.reshape(3, 3, CH, CH),
        conv_bias.reshape(1, CH),
        temporal_weight,
    ]
    outs = pl.pallas_call(
        kernel,
        out_shape=tuple(pltpu.VMEM(shape, kind) for shape, kind in shapes[:2] + [((12, 8, CH), F32), shapes[4]]),
        in_specs=[any_spec] * 8,
        out_specs=(any_spec,) * 4,
        scratch_shapes=[pltpu.VMEM(shape, kind) for shape, kind in scratch]
        + [
            pltpu.SemaphoreType.DMA((5,)),
            pltpu.SemaphoreType.DMA((len(LEAVE),)),
            pltpu.SemaphoreType.DMA((len(ARRIVE),)),
            pltpu.SemaphoreType.REGULAR((2,)),
        ],
        compiler_params=pltpu.CompilerParams(
            collective_id=0, has_side_effects=True, vmem_limit_bytes=40 << 20
        ),
        name="video_block_backward",
    )(*[pltpu.with_memory_space_constraint(a, pltpu.HBM) for a in operands])
    outs = pl.pallas_call(
        write_out,
        out_shape=tuple(jax.ShapeDtypeStruct(shape, kind) for shape, kind in shapes),
        in_specs=[any_spec] * 4,
        out_specs=(any_spec,) * 5,
        scratch_shapes=[pltpu.SemaphoreType.DMA((5,))],
        compiler_params=pltpu.CompilerParams(vmem_limit_bytes=1 << 20),
        name="write_out",
    )(*outs)
    return (outs[0].reshape(1, 1, COLS, CH), outs[1].reshape(1, HEAD, CH), outs[2], outs[3], outs[4])


def solution(mesh):
    return jax.shard_map(
        body,
        mesh=mesh,
        in_specs=(
            P("frame", "row", None, None),
            P("row", "frame", None),
            P("frame", "row", None, None),
            P("row", "frame", None),
            P(),
            P(),
            P(),
            P(),
        ),
        out_specs=(
            P("frame", "row", None, None),
            P("row", "frame", None),
            P(None, "row", None),
            P(None, "row", None),
            P(None, "row"),
        ),
        check_vma=False,
    )
```
